512 devices in a mesh: fibre: 64 (over z, x, core), tm: 8 (over y).
Axes of the slice: x: 4, y: 8, z: 8, core: 2. Of those that a mesh axis runs over, the one named last changes fastest.
Arguments:
- traces: bfloat16 [8192, 8192], P('fibre', 'tm'), may hold values from -6 to 6
- stack_weights: bfloat16 [65536, 2048], P('fibre'), may hold values from -0.125 to 0.125
- channel_lists: int32 [64, 64], P('fibre'), may hold values from 0 to 255, as said below
- lag_offsets: int32 [64, 64], P('fibre'), may hold values from 0 to 127
- lengths: int32 [64], P('fibre'), may hold values from 16 to 64, as said below
- class_weights: float32 [256, 4], replicated, may hold values from -0.375 to 0.375
- class_bias: float32 [4], replicated, may hold values from -4 to 4
Outputs:
- log_power: float32 [256, 256], P('fibre')
- logits: float32 [256, 4], P('fibre')
The draws below stay inside these ranges and needn't reach their ends.
Inputs may be any that keep to these rules, and one draw needn't show every extreme that they name: `channel_lists`: in each row, the values divided by 4 (rounded down) form a permutation of 0 to 63: each region reads exactly one channel block held by each index of fibre. `lengths`: some region has all 64 slots live.
All inputs are finite; a program needn't handle non-finite values.
Results may differ from the reference program's by a relative error of at most 0.0003.
Values may be sent and summed in bfloat16 or wider, within the bound.
A program may use at most 128 MiB of HBM per device.

```python
import jax
import jax.numpy as jnp
from jax import lax

BLOCK_CH = 32
BLOCKS_DEV = 4
MAX_LAG = 128
SRC_BLOCK = 256
BLOCKS_REG = 4
CLASSES = 4
LIST_LEN = 64
REGIONS = 64
SOURCE_BLOCKS = 256
CH_BLOCKS = 256
CHANNELS = 8192
SAMPLES = 8192


def draw_channel_lists(key, part):
    key = jax.random.fold_in(key, 11)
    keys = jax.random.split(key, REGIONS + 1)
    owners = jax.vmap(lambda single: jax.random.permutation(single, LIST_LEN))(keys[:REGIONS])
    within = jax.random.randint(keys[REGIONS], (REGIONS, LIST_LEN), 0, BLOCKS_DEV)
    return (owners.astype(jnp.int32) * BLOCKS_DEV + within).astype(jnp.int32)


def draw_lag_offsets(key, part):
    key = jax.random.fold_in(key, 23)
    first, second, third = jax.random.split(key, 3)
    values = jax.random.randint(first, (REGIONS, LIST_LEN), 0, MAX_LAG)
    row_pick = jax.random.randint(second, (), 0, REGIONS)
    slot_pick = jax.random.randint(third, (), 0, LIST_LEN)
    return values.at[row_pick, slot_pick].set(MAX_LAG - 1).astype(jnp.int32)


def draw_lengths(key, part):
    key = jax.random.fold_in(key, 37)
    first, second = jax.random.split(key)
    values = jax.random.randint(first, (REGIONS,), LIST_LEN // 4, LIST_LEN + 1)
    row_pick = jax.random.randint(second, (), 0, REGIONS)
    return values.at[row_pick].set(LIST_LEN).astype(jnp.int32)


def block_levels(stream_key, dims, cuts, least, largest):
    factor_of, own = 1.0, jax.random.fold_in(stream_key, 6)
    for axis_at, parts in cuts:
        heights = jnp.exp(jax.random.uniform(jax.random.fold_in(own, axis_at), (parts,), jnp.float32, least / len(cuts), largest / len(cuts)))
        factor_of = factor_of * jnp.repeat(heights, dims[axis_at] // parts).reshape([-1 if axis == axis_at else 1 for axis in range(len(dims))])
    return factor_of


def normal_values(rng, extent, width, limit, pieces=(), kind=jnp.bfloat16):
    drawn = jax.random.normal(rng, extent, jnp.float32) * width
    if len(pieces) > 0:
        drawn = block_levels(rng, extent, pieces, -0.22, 0.18) * drawn
    return jnp.clip(drawn, min=-limit, max=limit).astype(kind)


def setup_inputs(seed: int = 0) -> dict:
    key_list = jax.random.split(jax.random.key(seed), 8)
    traces = normal_values(key_list[0], (CHANNELS, SAMPLES), 1.0, 6.0, ((0, 64), (1, 8)))
    stack_weights = normal_values(key_list[1], (SOURCE_BLOCKS * SRC_BLOCK, LIST_LEN * BLOCK_CH), (LIST_LEN * BLOCK_CH) ** -0.5, 0.125, ((0, 64),))
    channel_lists = draw_channel_lists(jax.random.fold_in(key_list[7], 71), 0)
    lag_offsets = draw_lag_offsets(jax.random.fold_in(key_list[7], 71), 0)
    lengths = draw_lengths(jax.random.fold_in(key_list[7], 71), 0)
    class_weights = normal_values(key_list[5], (SRC_BLOCK, CLASSES), SRC_BLOCK ** -0.5, 0.375, (), jnp.float32)
    class_bias = normal_values(key_list[6], (CLASSES,), 1.0, 4.0, (), jnp.float32)
    return dict(traces=traces, stack_weights=stack_weights, channel_lists=channel_lists, lag_offsets=lag_offsets, lengths=lengths, class_weights=class_weights, class_bias=class_bias)


def region_power(extended, weights, slot_list, slot_offsets, length):
    zero_index = jnp.zeros((), jnp.int32)

    def cut_window(block_index, offset):
        return lax.dynamic_slice(extended, (block_index.astype(jnp.int32), zero_index, offset.astype(jnp.int32)), (1, BLOCK_CH, SAMPLES))[0]

    windows = jax.vmap(cut_window)(slot_list, slot_offsets)
    live_mask = (jnp.arange(LIST_LEN, dtype=jnp.int32) < length).astype(windows.dtype)
    windows = windows * live_mask[:, None, None]
    beams = jnp.dot(weights, windows.reshape(LIST_LEN * BLOCK_CH, SAMPLES), preferred_element_type=jnp.float32)
    beam_power = jnp.sum(beams * beams, axis=1) / SAMPLES
    return jnp.log(beam_power + 1e-6)


def reference(traces, stack_weights, channel_lists, lag_offsets, lengths, class_weights, class_bias):
    blocks = traces.reshape(CH_BLOCKS, BLOCK_CH, SAMPLES)
    padding = jnp.zeros((CH_BLOCKS, BLOCK_CH, MAX_LAG), traces.dtype)
    extended = jnp.concatenate([blocks, padding], axis=2)
    weights = stack_weights.reshape(REGIONS, BLOCKS_REG * SRC_BLOCK, LIST_LEN * BLOCK_CH)
    region_logs = lax.map(lambda items: region_power(extended, *items), (weights, channel_lists, lag_offsets, lengths))
    log_power = region_logs.reshape(SOURCE_BLOCKS, SRC_BLOCK)
    logits = jnp.dot(log_power, class_weights, precision=lax.Precision.HIGHEST) + class_bias
    return log_power, logits
```

```python
import functools

import jax
import jax.numpy as jnp
from jax import lax
from jax.experimental import pallas as pl
from jax.experimental.pallas import tpu as pltpu
from jax.sharding import PartitionSpec as P

BLOCK_CH = 32
MAX_LAG = 128
SRC_BLOCK = 256
NX = 4
MESH = pl.DeviceIdType.MESH


def kernel(nz, ny, samples, tab_ref, key_ref, traces_ref, w_ref, cw_ref, cb_ref, lp_ref, lg_ref, *scratch):
    nf = nz // 2
    nb = nz - 1 - nf
    labels = [("o", 0)]
    for h in range(1, nf + 1):
        labels.append(("f", h))
        if h <= nb:
            labels.append(("b", h))
    at = {label: i for i, label in enumerate(labels)}
    gz = scratch[:nz]
    gx = scratch[nz : 2 * nz]
    (
        tiles, stage, w_v, perm_v, wp_v, acc, tabs_v, tabs_s, ebuf,
        loc_sem, halo_sem, tab_send, tab_recv, smem_sem,
        z_send, z_recv, x_send, x_recv, t_send, t_recv, y_send, y_recv,
    ) = scratch[2 * nz :]
    seg = traces_ref.shape[2]
    rows = w_ref.shape[0]
    depth = w_ref.shape[1]
    chunk = 2 * NX * BLOCK_CH

    me = lax.axis_index("fibre")
    y = lax.axis_index("tm")
    c = lax.rem(me, 2)
    x = lax.rem(me // 2, NX)
    z = me // (2 * NX)
    d = 1 - 2 * c
    e = 1 - c

    def dev(zz, xx, cc):
        return {"fibre": (lax.rem(zz + 2 * nz, nz) * NX + lax.rem(xx + 2 * NX, NX)) * 2 + cc}

    def zoff(label):
        kind, h = label
        return {"o": 0, "f": -d * h, "b": d * h}[kind]

    def tslot(label):
        return lax.rem(zoff(label) + nz, nz)

    def col(xx, cc):
        return lax.rem(xx + 2 * NX, NX) * 2 + cc

    sibling = dev(z, x, e)
    fore, back = dev(z, x + d, c), dev(z, x - d, c)
    fore_e, back_e = dev(z, x + d, e), dev(z, x - d, e)
    zfore, zback = dev(z + d, x, c), dev(z - d, x, c)
    peers = [sibling, fore, back, fore_e, back_e]
    ring = [zfore, zback] if nb else [zfore]
    others = [{"tm": lax.rem(y + k, ny)} for k in range(1, ny)]

    barrier = pltpu.get_barrier_semaphore()
    for peer in peers + ring + others:
        pl.semaphore_signal(barrier, inc=1, device_id=peer, device_id_type=MESH)
    pl.semaphore_wait(barrier, len(peers) + len(ring) + len(others))

    def remote(src, dst, ssem, rsem, device):
        return pltpu.make_async_remote_copy(
            src_ref=src, dst_ref=dst, send_sem=ssem, recv_sem=rsem, device_id=device, device_id_type=MESH
        )

    own = gz[0]
    halo = remote(
        traces_ref.at[:, :, pl.ds(0, MAX_LAG)], own.at[:, :, pl.ds(seg, MAX_LAG)],
        halo_sem.at[0], halo_sem.at[1], {"tm": lax.rem(y + ny - 1, ny)},
    )
    if ny > 1:
        @pl.when(y > 0)
        def _():
            halo.start()
    own_copy = pltpu.make_async_copy(traces_ref, own.at[:, :, pl.ds(0, seg)], loc_sem.at[0])
    own_copy.start()
    slots = [1, 2, 4, 5, 3]
    tab_copies = [
        remote(tab_ref, tabs_v.at[slot], tab_send.at[i], tab_recv.at[slot], peer)
        for i, (slot, peer) in enumerate(zip(slots, peers))
    ]
    for copy in tab_copies:
        copy.start()
    w_copy = pltpu.make_async_copy(w_ref, w_v, loc_sem.at[1])
    w_copy.start()
    tabs_v[0] = tab_ref[...]

    @pl.when(y == ny - 1)
    def _():
        own[:, :, seg:] = jnp.zeros((own.shape[0], BLOCK_CH, MAX_LAG), jnp.bfloat16)

    own_copy.wait()
    if ny > 1:
        @pl.when(y < ny - 1)
        def _():
            halo.wait_recv()

    sent = []

    def start(copy):
        copy.start()
        sent.append(copy)

    def pass_along(label):
        kind, h = label
        i = at[label]
        if kind in "of" and h < nf:
            n = at[("f", h + 1)]
            start(remote(gz[i], gz[n], z_send.at[n], z_recv.at[n], zfore))
        if kind in "ob" and h < nb:
            n = at[("b", h + 1)]
            start(remote(gz[i], gz[n], z_send.at[n], z_recv.at[n], zback))
        start(remote(gz[i], gx[i], x_send.at[i], x_recv.at[i], fore))

    lane = lax.broadcasted_iota(jnp.int32, (BLOCK_CH, MAX_LAG), 1)

    def cut(src, region, owner, dst):
        word = tabs_s[region, 0, owner]
        block = lax.bitwise_and(word, 3)
        lag = lax.shift_right_logical(word, 2)
        turn = lax.bitwise_and(MAX_LAG - lag, MAX_LAG - 1)
        near = lane < MAX_LAG - lag
        held = pltpu.roll(src[block, :, 0:MAX_LAG].astype(jnp.float32), turn, 1)
        for j in range(seg // MAX_LAG):
            following = pltpu.roll(
                src[block, :, (j + 1) * MAX_LAG : (j + 2) * MAX_LAG].astype(jnp.float32), turn, 1
            )
            dst[:, j * MAX_LAG : (j + 1) * MAX_LAG] = jnp.where(near, held, following).astype(jnp.bfloat16)
            held = following

    def deal(src, label, xo, regions, base):
        t = tslot(label)
        owner = lax.rem(z + zoff(label) + nz, nz) * 2 * NX + col(xo, c)
        k = col(xo, c)
        for j, (region, peer) in enumerate(regions):
            n = base + j
            cut(src, region, owner, stage.at[n])
            start(remote(stage.at[n], tiles.at[t, k], t_send.at[n], t_recv.at[t, k], peer))
        cut(src, 0, owner, tiles.at[t, k])

    def near_tiles(label):
        deal(gz[at[label]], label, x, [(2, back), (3, back_e), (1, sibling)], 6 * at[label])

    def far_tiles(label):
        deal(gx[at[label]], label, x - d, [(4, fore), (5, fore_e), (1, sibling)], 6 * at[label] + 3)

    def wait_z(label):
        i = at[label]
        remote(gz[i], gz[i], z_send.at[i], z_recv.at[i], zfore).wait_recv()

    def wait_x(label):
        i = at[label]
        remote(gx[i], gx[i], x_send.at[i], x_recv.at[i], fore).wait_recv()

    def wait_tiles(label):
        t = tslot(label)
        ks = [col(x + d, c), col(x + 2, c), col(x, e), col(x + d, e), col(x - d, e), col(x + 2, e)]
        for k in ks:
            remote(stage.at[0], tiles.at[t, k], t_send.at[0], t_recv.at[t, k], fore).wait_recv()

    def arrange(label):
        i = at[label]
        first = lax.rem(z + zoff(label) + nz, nz) * chunk
        for kk in range(depth // chunk):
            wanted = lax.broadcasted_iota(jnp.int32, (chunk, chunk), 0) + first
            hit = key_ref[0:1, kk * chunk : (kk + 1) * chunk] == wanted
            perm_v[:, kk * chunk : (kk + 1) * chunk] = jnp.where(hit, 1.0, 0.0).astype(jnp.bfloat16)
        step = min(rows, 256)

        def body(r, carry):
            at_row = pl.multiple_of(r * step, step)
            wp_v[i, pl.ds(at_row, step), :] = lax.dot_general(
                w_v[pl.ds(at_row, step), :], perm_v[...], (((1,), (1,)), ((), ())),
                preferred_element_type=jnp.float32,
            ).astype(jnp.bfloat16)
            return carry

        lax.fori_loop(0, rows // step, body, 0)

    width = min(seg, 256)

    def add_chunk(label, first):
        t = tslot(label)
        i = at[label]

        def body(n, carry):
            cols = pl.ds(pl.multiple_of(n * width, width), width)
            part = jnp.dot(
                wp_v[i], tiles[t, :, :, cols].reshape(chunk, width), preferred_element_type=jnp.float32
            )
            acc[n] = part if first else acc[n] + part
            return carry

        lax.fori_loop(0, seg // width, body, 0)

    pass_along(labels[0])
    for slot, peer in zip(slots, peers):
        remote(tab_ref, tabs_v.at[slot], tab_send.at[0], tab_recv.at[slot], peer).wait_recv()
    to_smem = pltpu.make_async_copy(tabs_v, tabs_s, smem_sem)
    to_smem.start()
    to_smem.wait()
    near_tiles(labels[0])
    w_copy.wait()

    z_queue = list(labels[1:])
    x_queue = list(labels)
    chunks_left = list(labels)
    arrange_left = list(labels)
    done_x = []

    def step_z():
        label = z_queue.pop(0)
        wait_z(label)
        pass_along(label)
        near_tiles(label)

    def step_x():
        label = x_queue.pop(0)
        wait_x(label)
        far_tiles(label)
        done_x.append(label)

    def step_chunk():
        label = chunks_left.pop(0)
        wait_tiles(label)
        add_chunk(label, label == labels[0])

    while z_queue or x_queue:
        if arrange_left:
            arrange(arrange_left.pop(0))
        if z_queue:
            step_z()
        if z_queue:
            step_z()
        if x_queue:
            step_x()
        if len(done_x) > 1 and len(chunks_left) > len(labels) - len(done_x) + 1:
            step_chunk()
    while arrange_left:
        arrange(arrange_left.pop(0))
    while chunks_left:
        step_chunk()

    block = 128
    for r in range(rows // block):
        total = jnp.zeros((block, 128), jnp.float32)
        for n in range(seg // width):
            for j in range(width // 128):
                part = acc[n, r * block : (r + 1) * block, j * 128 : (j + 1) * 128]
                total = total + part * part
        ebuf[y, r : r + 1, :] = jnp.sum(total.T, axis=0, keepdims=True)

    for k, peer in enumerate(others):
        start(remote(ebuf.at[y], ebuf.at[y], y_send.at[k], y_recv.at[y], peer))
    for k in range(1, ny):
        source = lax.rem(y + k, ny)
        remote(ebuf.at[source], ebuf.at[source], y_send.at[0], y_recv.at[source], others[0]).wait_recv()
    energy = ebuf[0]
    for k in range(1, ny):
        energy = energy + ebuf[k]
    log_power = jnp.log(energy / samples + 1e-06)
    per = SRC_BLOCK // block
    for r in range(rows // block):
        lp_ref[r // per : r // per + 1, (r % per) * block : (r % per + 1) * block] = log_power[r : r + 1, :]
    lg_ref[...] = (
        jnp.dot(lp_ref[...], cw_ref[...], precision=lax.Precision.HIGHEST, preferred_element_type=jnp.float32)
        + cb_ref[...]
    )
    for copy in sent:
        copy.wait_send()
    for copy in tab_copies:
        copy.wait_send()
    if ny > 1:
        @pl.when(y > 0)
        def _():
            halo.wait_send()


def per_device(nz, ny, traces, stack_weights, channel_lists, lag_offsets, lengths, class_weights, class_bias):
    blocks = traces.shape[0] // BLOCK_CH
    seg = traces.shape[1]
    rows, depth = stack_weights.shape
    count = channel_lists.shape[1]
    chunk = 2 * NX * BLOCK_CH
    owners = channel_lists[0] // blocks
    slot = jnp.arange(count, dtype=jnp.int32)
    word = channel_lists[0] % blocks + 4 * lag_offsets[0]
    table = jnp.sum(jnp.where(owners[:, None] == jnp.arange(128, dtype=jnp.int32)[None, :], word[:, None], 0), axis=0)
    table = jnp.broadcast_to(table[None, :], (8, 128))
    keyed = jnp.where(
        (slot < lengths[0])[:, None], owners[:, None] * BLOCK_CH + jnp.arange(BLOCK_CH, dtype=jnp.int32)[None, :], -1
    )
    key = jnp.broadcast_to(keyed.reshape(1, depth), (8, depth))
    bf16, f32 = jnp.bfloat16, jnp.float32
    vmem = pl.BlockSpec(memory_space=pltpu.VMEM)
    hbm = pl.BlockSpec(memory_space=pl.ANY)
    dma = pltpu.SemaphoreType.DMA
    width = min(seg, 256)
    scratch = [pltpu.VMEM((blocks, BLOCK_CH, seg + MAX_LAG), bf16) for _ in range(2 * nz)] + [
        pltpu.VMEM((nz, 2 * NX, BLOCK_CH, seg), bf16),
        pltpu.VMEM((6 * nz, BLOCK_CH, seg), bf16),
        pltpu.VMEM((rows, depth), bf16),
        pltpu.VMEM((chunk, depth), bf16),
        pltpu.VMEM((nz, rows, chunk), bf16),
        pltpu.VMEM((seg // width, rows, width), f32),
        pltpu.VMEM((6, 8, 128), jnp.int32),
        pltpu.SMEM((6, 8, 128), jnp.int32),
        pltpu.VMEM((ny, rows // 128, 128), f32),
        dma((2,)), dma((2,)), dma((5,)), dma((6,)), dma,
        dma((nz,)), dma((nz,)), dma((nz,)), dma((nz,)), dma((6 * nz,)), dma((nz, 2 * NX)), dma((ny,)), dma((ny,)),
    ]
    return pl.pallas_call(
        functools.partial(kernel, nz, ny, float(seg * ny)),
        out_shape=(
            jax.ShapeDtypeStruct((rows // SRC_BLOCK, SRC_BLOCK), f32),
            jax.ShapeDtypeStruct((rows // SRC_BLOCK, class_weights.shape[1]), f32),
        ),
        in_specs=[vmem, vmem, hbm, hbm, vmem, vmem],
        out_specs=(vmem, vmem),
        scratch_shapes=scratch,
        compiler_params=pltpu.CompilerParams(
            collective_id=0, has_side_effects=True, vmem_limit_bytes=56 * 1024 * 1024
        ),
    )(table, key, traces.reshape(blocks, BLOCK_CH, seg), stack_weights, class_weights, class_bias.reshape(1, -1))


def solution(mesh):
    placed = (
        P("fibre", "tm"),
        P("fibre", None),
        P("fibre", None),
        P("fibre", None),
        P("fibre"),
        P(),
        P(),
    )
    nz = mesh.shape["fibre"] // (2 * NX)
    return jax.shard_map(
        functools.partial(per_device, nz, mesh.shape["tm"]),
        mesh=mesh,
        in_specs=placed,
        out_specs=(P("fibre", None), P("fibre", None)),
        check_vma=False,
    )
```

```python
import functools

import jax
import jax.numpy as jnp
from jax import lax
from jax.experimental import pallas as pl
from jax.experimental.pallas import tpu as pltpu
from jax.sharding import PartitionSpec as P

BLOCK_CH = 32
MAX_LAG = 128
SRC_BLOCK = 256
NX = 4
HALF = BLOCK_CH // 2
MESH = pl.DeviceIdType.MESH


def kernel(
    nz, ny, samples, list_ref, lag_ref, len_ref, traces_ref, w_ref, cw_ref, cb_ref, lp_ref, lg_ref, *scratch
):
    nf = nz // 2
    nb = nz - 1 - nf
    labels = [("o", 0)]
    for h in range(1, nf + 1):
        labels.append(("f", h))
        if h <= nb:
            labels.append(("b", h))
    at = {label: i for i, label in enumerate(labels)}
    gz = scratch[:nz]
    gx = scratch[nz : 2 * nz]
    (
        tiles, full, half, w_v, perm_v, wp_v, acc, pad, tab_v, tabs_v, tabs_s, ebuf,
        loc_sem, halo_sem, tab_send, tab_recv, smem_sem,
        z_send, z_recv, x_send, x_recv, f_send, h_send, t_recv, y_send, y_recv,
    ) = scratch[2 * nz :]
    seg = traces_ref.shape[2]
    rows = w_ref.shape[0]
    depth = w_ref.shape[1]
    count = list_ref.shape[1]
    chunk = 2 * NX * BLOCK_CH

    me = lax.axis_index("fibre")
    y = lax.axis_index("tm")
    c = lax.rem(me, 2)
    x = lax.rem(me // 2, NX)
    z = me // (2 * NX)
    d = 1 - 2 * c
    e = 1 - c

    def dev(zz, xx, cc):
        return {"fibre": (lax.rem(zz + 2 * nz, nz) * NX + lax.rem(xx + 2 * NX, NX)) * 2 + cc}

    def zoff(label):
        kind, h = label
        return {"o": 0, "f": -d * h, "b": d * h}[kind]

    def tslot(label):
        return lax.rem(zoff(label) + nz, nz)

    def col(xx, cc):
        return lax.rem(xx + 2 * NX, NX) * 2 + cc

    sibling = dev(z, x, e)
    peers = [sibling] + [dev(z, x + s, cc) for s in (1, -1, 2) for cc in (c, e)]
    slots = [1, 4, 5, 2, 3, 6, 7]
    opposite = peers[5]
    zfore, zback = dev(z + d, x, c), dev(z - d, x, c)
    ring = [zfore, zback] if nb else [zfore]
    others = [{"tm": lax.rem(y + k, ny)} for k in range(1, ny)]

    barrier = pltpu.get_barrier_semaphore()
    for peer in peers + ring + others:
        pl.semaphore_signal(barrier, inc=1, device_id=peer, device_id_type=MESH)
    pl.semaphore_wait(barrier, len(peers) + len(ring) + len(others))

    def remote(src, dst, ssem, rsem, device):
        return pltpu.make_async_remote_copy(
            src_ref=src, dst_ref=dst, send_sem=ssem, recv_sem=rsem, device_id=device, device_id_type=MESH
        )

    sent = []

    def start(copy):
        copy.start()
        sent.append(copy)

    own = gz[0]
    hi = pl.ds(HALF, HALF)
    main, rim = pl.ds(0, seg), pl.ds(seg, MAX_LAG)
    halo = remote(
        traces_ref.at[:, :, pl.ds(0, MAX_LAG)], own.at[:, :, rim],
        halo_sem.at[0], halo_sem.at[1], {"tm": lax.rem(y + ny - 1, ny)},
    )
    if ny > 1:
        @pl.when(y > 0)
        def _():
            halo.start()
    firsts = [(at[("f", 1)], zfore)] + ([(at[("b", 1)], zback)] if nb else [])
    for n, peer in firsts:
        start(remote(traces_ref, gz[n].at[:, :, main], z_send.at[n, 0], z_recv.at[n, 0], peer))
    start(remote(traces_ref.at[:, hi], gx[0].at[:, :, main], x_send.at[0, 0], x_recv.at[0, 0], opposite))
    own_copy = pltpu.make_async_copy(traces_ref, own.at[:, :, main], loc_sem.at[0])
    own_copy.start()
    w_copy = pltpu.make_async_copy(w_ref, w_v, loc_sem.at[1])
    w_copy.start()

    @pl.when(y == ny - 1)
    def _():
        own[:, :, seg:] = jnp.zeros((own.shape[0], BLOCK_CH, MAX_LAG), jnp.bfloat16)

    pad[...] = jnp.zeros_like(pad)
    pad[0:1, 0:count] = list_ref[...] + 256 * lag_ref[...]
    asked = jnp.broadcast_to(pad[0:1, :], (128, 128)).T[0:count, :]
    owner_of = lax.shift_right_logical(lax.bitwise_and(asked, 255), 2)
    word = lax.bitwise_or(
        lax.bitwise_and(asked, 3), lax.shift_left(lax.shift_right_logical(asked, 8), 2)
    )
    wanted = lax.broadcasted_iota(jnp.int32, (count, 128), 1)
    table = jnp.sum(jnp.where(owner_of == wanted, word, 0), axis=0, keepdims=True)
    tab_v[...] = jnp.broadcast_to(table, (8, 128))
    tabs_v[0] = tab_v[...]
    for i, (slot, peer) in enumerate(zip(slots, peers)):
        start(remote(tab_v, tabs_v.at[slot], tab_send.at[i], tab_recv.at[slot], peer))

    live = lax.broadcasted_iota(jnp.int32, (1, count), 1) < len_ref[...]
    keyed = jnp.where(live, lax.shift_right_logical(list_ref[...], 2), 2 * nz * NX)
    spread = lax.shift_right_logical(lax.broadcasted_iota(jnp.int32, (count, depth), 1), 5)
    spread = spread == lax.broadcasted_iota(jnp.int32, (count, depth), 0)
    key = jnp.dot(
        jnp.broadcast_to(keyed, (8, count)).astype(jnp.float32).astype(jnp.bfloat16),
        jnp.where(spread, 1.0, 0.0).astype(jnp.bfloat16),
        preferred_element_type=jnp.float32,
    )
    inner = lax.bitwise_and(lax.broadcasted_iota(jnp.int32, (1, depth), 1), BLOCK_CH - 1)
    key = key[0:1, :].astype(jnp.int32) * BLOCK_CH + inner

    def arrange(label):
        i = at[label]
        first = lax.rem(z + zoff(label) + nz, nz) * chunk
        target = lax.broadcasted_iota(jnp.int32, (chunk, chunk), 0) + first
        for kk in range(depth // chunk):
            hit = key[:, kk * chunk : (kk + 1) * chunk] == target
            perm_v[:, kk * chunk : (kk + 1) * chunk] = jnp.where(hit, 1.0, 0.0).astype(jnp.bfloat16)
        step = min(rows, 256)

        def body(r, carry):
            at_row = pl.multiple_of(r * step, step)
            wp_v[i, pl.ds(at_row, step), :] = lax.dot_general(
                w_v[pl.ds(at_row, step), :], perm_v[...], (((1,), (1,)), ((), ())),
                preferred_element_type=jnp.float32,
            ).astype(jnp.bfloat16)
            return carry

        lax.fori_loop(0, rows // step, body, 0)

    def pass_along(label):
        kind, h = label
        i = at[label]
        if kind == "f" and h < nf:
            n = at[("f", h + 1)]
            start(remote(gz[i], gz[n], z_send.at[n, 0], z_recv.at[n, 0], zfore))
        if kind == "b" and h < nb:
            n = at[("b", h + 1)]
            start(remote(gz[i], gz[n], z_send.at[n, 0], z_recv.at[n, 0], zback))

    def pass_along_hi(label):
        kind, h = label
        i = at[label]
        if kind in "of" and h < nf:
            n = at[("f", h + 1)]
            start(remote(gx[i], gx[n], x_send.at[n, 0], x_recv.at[n, 0], zfore))
        if kind in "ob" and h < nb:
            n = at[("b", h + 1)]
            start(remote(gx[i], gx[n], x_send.at[n, 0], x_recv.at[n, 0], zback))

    def cut(src, height, region, owner, dst):
        lane = lax.broadcasted_iota(jnp.int32, (height, MAX_LAG), 1)
        word = tabs_s[region, 0, owner]
        block = lax.bitwise_and(word, 3)
        lag = lax.shift_right_logical(word, 2)
        turn = lax.bitwise_and(MAX_LAG - lag, MAX_LAG - 1)
        near = lane < MAX_LAG - lag
        held = pltpu.roll(src[block, 0:height, 0:MAX_LAG].astype(jnp.float32), turn, 1)
        for j in range(seg // MAX_LAG):
            following = pltpu.roll(
                src[block, 0:height, (j + 1) * MAX_LAG : (j + 2) * MAX_LAG].astype(jnp.float32), turn, 1
            )
            dst[:, j * MAX_LAG : (j + 1) * MAX_LAG] = jnp.where(near, held, following).astype(jnp.bfloat16)
            held = following

    def owner_at(label, xx):
        return lax.rem(z + zoff(label) + nz, nz) * 2 * NX + col(xx, c)

    def near_tiles(label):
        i = at[label]
        t = tslot(label)
        k = col(x, c)
        owner = owner_at(label, x)
        for j in range(4):
            n = 5 * i + j
            cut(gz[i], BLOCK_CH, 2 + j, owner, full.at[n])
            start(remote(full.at[n], tiles.at[t, k], f_send.at[n], t_recv.at[t, k, 0], peers[1 + j]))
        for j in range(2):
            n = 3 * i + j
            cut(gz[i], HALF, 6 + j, owner, half.at[n])
            start(
                remote(half.at[n], tiles.at[t, k, pl.ds(0, HALF)], h_send.at[n], t_recv.at[t, k, 0], peers[5 + j])
            )
        n = 5 * i + 4
        cut(gz[i], BLOCK_CH, 1, owner, full.at[n])
        start(remote(full.at[n], tiles.at[t, k], f_send.at[n], t_recv.at[t, k, 0], sibling))
        cut(gz[i], BLOCK_CH, 0, owner, tiles.at[t, k])

    def hi_tiles(label):
        i = at[label]
        t = tslot(label)
        k = col(x + 2, c)
        owner = owner_at(label, x + 2)
        n = 3 * i + 2
        cut(gx[i], HALF, 1, owner, half.at[n])
        start(remote(half.at[n], tiles.at[t, k, hi], h_send.at[n], t_recv.at[t, k, 1], sibling))
        cut(gx[i], HALF, 0, owner, tiles.at[t, k, hi])

    def wait_z(label):
        i = at[label]
        if label[1] == 1:
            for part, cols in enumerate((main, rim)):
                dst = gz[i].at[:, :, cols]
                remote(dst, dst, z_send.at[i, part], z_recv.at[i, part], zfore).wait_recv()
        else:
            remote(gz[i], gz[i], z_send.at[i, 0], z_recv.at[i, 0], zfore).wait_recv()

    def wait_hi(label):
        i = at[label]
        if label[1] == 0:
            for part, cols in enumerate((main, rim)):
                dst = gx[i].at[:, :, cols]
                remote(dst, dst, x_send.at[i, part], x_recv.at[i, part], zfore).wait_recv()
        else:
            remote(gx[i], gx[i], x_send.at[i, 0], x_recv.at[i, 0], zfore).wait_recv()

    def wait_tiles(label):
        t = tslot(label)
        for k in (col(x, e), col(x + 1, c), col(x + 1, e), col(x - 1, c), col(x - 1, e)):
            remote(full.at[0], tiles.at[t, k], f_send.at[0], t_recv.at[t, k, 0], sibling).wait_recv()
        for cc in (c, e):
            k = col(x + 2, cc)
            dst = tiles.at[t, k, pl.ds(0, HALF)]
            remote(half.at[0], dst, h_send.at[0], t_recv.at[t, k, 0], sibling).wait_recv()
        k = col(x + 2, e)
        remote(half.at[0], tiles.at[t, k, hi], h_send.at[0], t_recv.at[t, k, 1], sibling).wait_recv()

    width = min(seg, 256)

    def add_chunk(label):
        t = tslot(label)
        i = at[label]
        wait_tiles(label)

        def body(n, carry):
            cols = pl.ds(pl.multiple_of(n * width, width), width)
            part = jnp.dot(
                wp_v[i], tiles[t, :, :, cols].reshape(chunk, width), preferred_element_type=jnp.float32
            )
            acc[n] = part if i == 0 else acc[n] + part
            return carry

        lax.fori_loop(0, seg // width, body, 0)

    w_copy.wait()
    arrange(labels[0])
    if ny > 1:
        @pl.when(y < ny - 1)
        def _():
            halo.wait_recv()
    for n, peer in firsts:
        start(remote(own.at[:, :, rim], gz[n].at[:, :, rim], z_send.at[n, 1], z_recv.at[n, 1], peer))
    start(remote(own.at[:, hi, rim], gx[0].at[:, :, rim], x_send.at[0, 1], x_recv.at[0, 1], opposite))
    for slot, peer in zip(slots, peers):
        remote(tab_v, tabs_v.at[slot], tab_send.at[0], tab_recv.at[slot], peer).wait_recv()
    to_smem = pltpu.make_async_copy(tabs_v, tabs_s, smem_sem)
    to_smem.start()
    to_smem.wait()
    own_copy.wait()
    near_tiles(labels[0])

    by_hop = [[label for label in labels if label[1] == h] for h in range(nf + 1)]
    to_arrange = list(labels[1:])
    to_add = list(labels)
    for h in range(1, nf + 1):
        for label in by_hop[h]:
            wait_z(label)
            pass_along(label)
        for label in by_hop[h]:
            near_tiles(label)
        for label in by_hop[h - 1]:
            wait_hi(label)
            pass_along_hi(label)
            hi_tiles(label)
        for _ in range(2):
            if to_arrange:
                arrange(to_arrange.pop(0))
        if h >= 2:
            for _ in by_hop[h - 2]:
                add_chunk(to_add.pop(0))
    while to_arrange:
        arrange(to_arrange.pop(0))
    while len(to_add) > len(by_hop[nf]):
        add_chunk(to_add.pop(0))
    for label in by_hop[nf]:
        wait_hi(label)
        hi_tiles(label)
        add_chunk(label)

    block = 128
    for r in range(rows // block):
        total = jnp.zeros((block, 128), jnp.float32)
        for n in range(seg // width):
            for j in range(width // 128):
                part = acc[n, r * block : (r + 1) * block, j * 128 : (j + 1) * 128]
                total = total + part * part
        ebuf[y, r : r + 1, :] = jnp.sum(total.T, axis=0, keepdims=True)

    for k, peer in enumerate(others):
        start(remote(ebuf.at[y], ebuf.at[y], y_send.at[k], y_recv.at[y], peer))
    for k in range(1, ny):
        source = lax.rem(y + k, ny)
        remote(ebuf.at[source], ebuf.at[source], y_send.at[0], y_recv.at[source], others[0]).wait_recv()
    energy = ebuf[0]
    for k in range(1, ny):
        energy = energy + ebuf[k]
    log_power = jnp.log(energy / samples + 1e-06)
    per = SRC_BLOCK // block
    for r in range(rows // block):
        lp_ref[r // per : r // per + 1, (r % per) * block : (r % per + 1) * block] = log_power[r : r + 1, :]
    powers = lp_ref[...]
    classes = cw_ref.shape[0]
    place = lax.broadcasted_iota(jnp.int32, (powers.shape[0], classes), 1)
    scores = jnp.broadcast_to(cb_ref[...], place.shape)
    for j in range(classes):
        score = jnp.sum(powers * cw_ref[j : j + 1, :], axis=1, keepdims=True)
        scores = scores + jnp.where(place == j, score, 0.0)
    lg_ref[...] = scores
    for copy in sent:
        copy.wait_send()
    if ny > 1:
        @pl.when(y > 0)
        def _():
            halo.wait_send()


def per_device(nz, ny, traces, stack_weights, channel_lists, lag_offsets, lengths, class_weights, class_bias):
    blocks = traces.shape[0] // BLOCK_CH
    seg = traces.shape[1]
    rows, depth = stack_weights.shape
    chunk = 2 * NX * BLOCK_CH
    bf16, f32 = jnp.bfloat16, jnp.float32
    vmem = pl.BlockSpec(memory_space=pltpu.VMEM)
    hbm = pl.BlockSpec(memory_space=pl.ANY)
    dma = pltpu.SemaphoreType.DMA
    width = min(seg, 256)
    scratch = (
        [pltpu.VMEM((blocks, BLOCK_CH, seg + MAX_LAG), bf16) for _ in range(nz)]
        + [pltpu.VMEM((blocks, HALF, seg + MAX_LAG), bf16) for _ in range(nz)]
        + [
            pltpu.VMEM((nz, 2 * NX, BLOCK_CH, seg), bf16),
            pltpu.VMEM((5 * nz, BLOCK_CH, seg), bf16),
            pltpu.VMEM((3 * nz, HALF, seg), bf16),
            pltpu.VMEM((rows, depth), bf16),
            pltpu.VMEM((chunk, depth), bf16),
            pltpu.VMEM((nz, rows, chunk), bf16),
            pltpu.VMEM((seg // width, rows, width), f32),
            pltpu.VMEM((8, 128), jnp.int32),
            pltpu.VMEM((8, 128), jnp.int32),
            pltpu.VMEM((8, 8, 128), jnp.int32),
            pltpu.SMEM((8, 8, 128), jnp.int32),
            pltpu.VMEM((ny, rows // 128, 128), f32),
            dma((2,)), dma((2,)), dma((7,)), dma((8,)), dma,
            dma((nz, 2)), dma((nz, 2)), dma((nz, 2)), dma((nz, 2)),
            dma((5 * nz,)), dma((3 * nz,)), dma((nz, 2 * NX, 2)), dma((ny,)), dma((ny,)),
        ]
    )
    return pl.pallas_call(
        functools.partial(kernel, nz, ny, float(seg * ny)),
        out_shape=(
            jax.ShapeDtypeStruct((rows // SRC_BLOCK, SRC_BLOCK), f32),
            jax.ShapeDtypeStruct((rows // SRC_BLOCK, class_weights.shape[1]), f32),
        ),
        in_specs=[vmem, vmem, vmem, hbm, hbm, vmem, vmem],
        out_specs=(vmem, vmem),
        scratch_shapes=scratch,
        compiler_params=pltpu.CompilerParams(
            collective_id=0, has_side_effects=True, vmem_limit_bytes=56 * 1024 * 1024
        ),
    )(
        channel_lists, lag_offsets, lengths.reshape(1, 1), traces.reshape(blocks, BLOCK_CH, seg), stack_weights,
        class_weights.T, class_bias.reshape(1, -1),
    )


def solution(mesh):
    placed = (
        P("fibre", "tm"),
        P("fibre", None),
        P("fibre", None),
        P("fibre", None),
        P("fibre"),
        P(),
        P(),
    )
    nz = mesh.shape["fibre"] // (2 * NX)
    return jax.shard_map(
        functools.partial(per_device, nz, mesh.shape["tm"]),
        mesh=mesh,
        in_specs=placed,
        out_specs=(P("fibre", None), P("fibre", None)),
        check_vma=False,
    )
```

```python
import functools

import jax
import jax.numpy as jnp
from jax import lax
from jax.experimental import pallas as pl
from jax.experimental.pallas import tpu as pltpu
from jax.sharding import PartitionSpec as P

BLOCK_CH = 32
MAX_LAG = 128
SRC_BLOCK = 256
NX = 4
HALF = BLOCK_CH // 2
EARLY, LATER = 1, 2
MESH = pl.DeviceIdType.MESH


def kernel(
    nz, ny, list_hbm, lag_hbm, len_hbm, traces_ref, w_ref, energy_ref, *scratch
):
    nf = nz // 2
    nb = nz - 1 - nf
    labels = [("o", 0)]
    for h in range(1, nf + 1):
        labels.append(("f", h))
        if h <= nb:
            labels.append(("b", h))
    at = {label: i for i, label in enumerate(labels)}
    gz = scratch[:nz]
    gx = scratch[nz : 2 * nz]
    gs = scratch[2 * nz : 3 * nz]
    gsx = scratch[3 * nz : 4 * nz]
    (
        tiles, full, half, w_v, perm_v, wp_v, acc, squares, list_ref, lag_ref, len_ref, pad, tab_v, tabs_v, tabs_s, ebuf,
        loc_sem, halo_sem, tab_send, tab_recv, smem_sem,
        z_send, z_recv, x_send, x_recv, s_send, s_recv, sx_send, sx_recv, f_send, h_send, t_recv, y_send, y_recv,
    ) = scratch[4 * nz :]
    seg = traces_ref.shape[2]
    rows = w_ref.shape[0]
    depth = w_ref.shape[1]
    count = list_ref.shape[1]
    chunk = 2 * NX * BLOCK_CH

    me = lax.axis_index("fibre")
    y = lax.axis_index("tm")
    c = lax.rem(me, 2)
    x = lax.rem(me // 2, NX)
    z = me // (2 * NX)
    d = 1 - 2 * c
    e = 1 - c

    def dev(zz, xx, cc):
        return {"fibre": (lax.rem(zz + 2 * nz, nz) * NX + lax.rem(xx + 2 * NX, NX)) * 2 + cc}

    def zoff(label):
        kind, h = label
        return {"o": 0, "f": -d * h, "b": d * h}[kind]

    def tslot(label):
        return lax.rem(zoff(label) + nz, nz)

    def col(xx, cc):
        return lax.rem(xx + 2 * NX, NX) * 2 + cc

    sibling = dev(z, x, e)
    peers = [dev(z, x + s, c) for s in (1, -1, 2)]
    slots = [2, 1, 3]
    opposite = peers[2]
    zfore, zback = dev(z + d, x, c), dev(z - d, x, c)
    ring = [zfore, zback] if nb else [zfore]
    others = [{"tm": lax.rem(y + k, ny)} for k in range(1, ny)]

    fetched = [
        pltpu.make_async_copy(src, dst, loc_sem.at[2 + i])
        for i, (src, dst) in enumerate(((list_hbm, list_ref), (lag_hbm, lag_ref), (len_hbm, len_ref)))
    ]
    for copy in fetched:
        copy.start()
    own = gz[0]
    hi = pl.ds(HALF, HALF)
    main, rim = pl.ds(0, seg), pl.ds(seg, MAX_LAG)
    own_copy = pltpu.make_async_copy(traces_ref, own.at[:, :, main], loc_sem.at[0])
    own_copy.start()
    w_copy = pltpu.make_async_copy(w_ref, w_v, loc_sem.at[1])
    w_copy.start()
    barrier = pltpu.get_barrier_semaphore()
    near = [sibling] + peers + ring
    for peer in near + others:
        pl.semaphore_signal(barrier, inc=1, device_id=peer, device_id_type=MESH)
    for copy in fetched:
        copy.wait()
    pad[...] = jnp.zeros_like(pad)
    pad[0:1, 0:count] = list_ref[...] + 256 * lag_ref[...]
    asked = jnp.broadcast_to(pad[0:1, :], (128, 128)).T[0:count, :]
    owner_of = lax.shift_right_logical(lax.bitwise_and(asked, 255), 2)
    word = lax.bitwise_or(
        lax.bitwise_and(asked, 3), lax.shift_left(lax.shift_right_logical(asked, 8), 2)
    )
    wanted = lax.broadcasted_iota(jnp.int32, (count, 128), 1)
    table = jnp.sum(jnp.where(owner_of == wanted, word, 0), axis=0, keepdims=True)
    tab_v[...] = jnp.broadcast_to(table, (8, 128))
    tabs_v[0] = tab_v[...]
    live = lax.broadcasted_iota(jnp.int32, (1, count), 1) < len_ref[...]
    keyed = jnp.where(live, lax.shift_right_logical(list_ref[...], 2), 2 * nz * NX)
    spread = lax.shift_right_logical(lax.broadcasted_iota(jnp.int32, (count, depth), 1), 5)
    spread = spread == lax.broadcasted_iota(jnp.int32, (count, depth), 0)
    key = jnp.dot(
        jnp.broadcast_to(keyed, (8, count)).astype(jnp.float32).astype(jnp.bfloat16),
        jnp.where(spread, 1.0, 0.0).astype(jnp.bfloat16),
        preferred_element_type=jnp.float32,
    )
    inner = lax.bitwise_and(lax.broadcasted_iota(jnp.int32, (1, depth), 1), BLOCK_CH - 1)
    key = key[0:1, :].astype(jnp.int32) * BLOCK_CH + inner

    @pl.when(y == ny - 1)
    def _():
        own[:, :, seg:] = jnp.zeros((own.shape[0], BLOCK_CH, MAX_LAG), jnp.bfloat16)

    pl.semaphore_wait(barrier, len(near) + len(others))

    def remote(src, dst, ssem, rsem, device):
        return pltpu.make_async_remote_copy(
            src_ref=src, dst_ref=dst, send_sem=ssem, recv_sem=rsem, device_id=device, device_id_type=MESH
        )

    sent = []

    def start(copy):
        copy.start()
        sent.append(copy)

    halo = remote(
        traces_ref.at[:, :, pl.ds(0, MAX_LAG)], own.at[:, :, rim],
        halo_sem.at[0], halo_sem.at[1], {"tm": lax.rem(y + ny - 1, ny)},
    )
    if ny > 1:
        @pl.when(y > 0)
        def _():
            halo.start()
    firsts = [(at[("f", 1)], zfore)] + ([(at[("b", 1)], zback)] if nb else [])
    for n, peer in firsts:
        start(remote(traces_ref, gz[n].at[:, :, main], z_send.at[n, 0], z_recv.at[n, 0], peer))
    start(remote(traces_ref.at[:, hi], gx[0].at[:, :, main], x_send.at[0, 0], x_recv.at[0, 0], opposite))
    for i, (slot, peer) in enumerate(zip(slots, peers)):
        start(remote(tab_v, tabs_v.at[slot], tab_send.at[i], tab_recv.at[slot], peer))

    def arrange(label):
        i = at[label]
        first = lax.rem(z + zoff(label) + nz, nz) * chunk
        target = lax.broadcasted_iota(jnp.int32, (chunk, chunk), 0) + first
        for kk in range(depth // chunk):
            hit = key[:, kk * chunk : (kk + 1) * chunk] == target
            perm_v[:, kk * chunk : (kk + 1) * chunk] = jnp.where(hit, 1.0, 0.0).astype(jnp.bfloat16)
        step = min(rows, 256)

        def body(r, carry):
            at_row = pl.multiple_of(r * step, step)
            wp_v[i, pl.ds(at_row, step), :] = lax.dot_general(
                w_v[pl.ds(at_row, step), :], perm_v[...], (((1,), (1,)), ((), ())),
                preferred_element_type=jnp.float32,
            ).astype(jnp.bfloat16)
            return carry

        lax.fori_loop(0, rows // step, body, 0)

    def pass_along(label):
        kind, h = label
        i = at[label]
        if kind == "f" and h < nf:
            n = at[("f", h + 1)]
            start(remote(gz[i], gz[n], z_send.at[n, 0], z_recv.at[n, 0], zfore))
        if kind == "b" and h < nb:
            n = at[("b", h + 1)]
            start(remote(gz[i], gz[n], z_send.at[n, 0], z_recv.at[n, 0], zback))

    def pass_along_hi(label):
        kind, h = label
        i = at[label]
        if kind in "of" and h < nf:
            n = at[("f", h + 1)]
            start(remote(gx[i], gx[n], x_send.at[n, 0], x_recv.at[n, 0], zfore))
        if kind in "ob" and h < nb:
            n = at[("b", h + 1)]
            start(remote(gx[i], gx[n], x_send.at[n, 0], x_recv.at[n, 0], zback))

    def cut(src, height, region, owner, dst):
        lane = lax.broadcasted_iota(jnp.int32, (height, MAX_LAG), 1)
        word = tabs_s[region, 0, owner]
        block = lax.bitwise_and(word, 3)
        lag = lax.shift_right_logical(word, 2)
        turn = lax.bitwise_and(MAX_LAG - lag, MAX_LAG - 1)
        near = lane < MAX_LAG - lag
        held = pltpu.roll(src[block, 0:height, 0:MAX_LAG].astype(jnp.float32), turn, 1)
        for j in range(seg // MAX_LAG):
            following = pltpu.roll(
                src[block, 0:height, (j + 1) * MAX_LAG : (j + 2) * MAX_LAG].astype(jnp.float32), turn, 1
            )
            dst[:, j * MAX_LAG : (j + 1) * MAX_LAG] = jnp.where(near, held, following).astype(jnp.bfloat16)
            held = following

    def mirror(label):
        kind, h = label
        return {"o": ("o", 0), "f": ("b", h) if h <= nb else ("f", h), "b": ("f", h)}[kind]

    def swap(label):
        i = at[label]
        start(remote(gz[i], gs[i], s_send.at[i], s_recv.at[i], sibling))

    def swap_hi(label):
        i = at[label]
        start(remote(gx[i], gsx[i], sx_send.at[i], sx_recv.at[i], sibling))

    def near_tiles(label):
        i = at[label]
        t = tslot(label)
        m = at[mirror(label)]
        remote(gs[m], gs[m], s_send.at[m], s_recv.at[m], sibling).wait_recv()
        first = lax.rem(z + zoff(label) + nz, nz) * 2 * NX + 2 * x
        mine = pl.ds(2 * x, 2)
        for j in range(2):
            n = 2 * i + j
            cut(gz[i], BLOCK_CH, 1 + j, first + c, full.at[n, c])
            cut(gs[m], BLOCK_CH, 1 + j, first + e, full.at[n, e])
            start(remote(full.at[n], tiles.at[t, mine], f_send.at[n], t_recv.at[t, x], peers[j]))
        cut(gz[i], HALF, 3, first + c, half.at[i, c])
        cut(gs[m], HALF, 3, first + e, half.at[i, e])
        start(remote(half.at[i], tiles.at[t, mine, pl.ds(0, HALF)], h_send.at[i], t_recv.at[t, x], opposite))
        cut(gz[i], BLOCK_CH, 0, first + c, tiles.at[t, 2 * x + c])
        cut(gs[m], BLOCK_CH, 0, first + e, tiles.at[t, 2 * x + e])

    def hi_tiles(label):
        i = at[label]
        t = tslot(label)
        m = at[mirror(label)]
        remote(gsx[m], gsx[m], sx_send.at[m], sx_recv.at[m], sibling).wait_recv()
        there = col(x + 2, 0)
        first = lax.rem(z + zoff(label) + nz, nz) * 2 * NX + there
        cut(gx[i], HALF, 0, first + c, tiles.at[t, there + c, hi])
        cut(gsx[m], HALF, 0, first + e, tiles.at[t, there + e, hi])

    def wait_z(label):
        i = at[label]
        if label[1] == 1:
            for part, cols in enumerate((main, rim)):
                dst = gz[i].at[:, :, cols]
                remote(dst, dst, z_send.at[i, part], z_recv.at[i, part], zfore).wait_recv()
        else:
            remote(gz[i], gz[i], z_send.at[i, 0], z_recv.at[i, 0], zfore).wait_recv()

    def wait_hi(label):
        i = at[label]
        if label[1] == 0:
            for part, cols in enumerate((main, rim)):
                dst = gx[i].at[:, :, cols]
                remote(dst, dst, x_send.at[i, part], x_recv.at[i, part], zfore).wait_recv()
        else:
            remote(gx[i], gx[i], x_send.at[i, 0], x_recv.at[i, 0], zfore).wait_recv()

    def wait_tiles(label):
        t = tslot(label)
        for step in (1, -1):
            source = lax.rem(x + step + NX, NX)
            dst = tiles.at[t, pl.ds(2 * source, 2)]
            remote(full.at[0], dst, f_send.at[0], t_recv.at[t, source], sibling).wait_recv()
        source = lax.rem(x + 2, NX)
        dst = tiles.at[t, pl.ds(2 * source, 2), pl.ds(0, HALF)]
        remote(half.at[0], dst, h_send.at[0], t_recv.at[t, source], sibling).wait_recv()

    width = min(seg, 256)

    def add_chunk(label):
        t = tslot(label)
        i = at[label]
        wait_tiles(label)

        def body(n, carry):
            cols = pl.ds(pl.multiple_of(n * width, width), width)
            part = jnp.dot(
                wp_v[i], tiles[t, :, :, cols].reshape(chunk, width), preferred_element_type=jnp.float32
            )
            if i > 0:
                part = acc[n] + part
            if i < nz - 1:
                acc[n] = part
            else:
                part = part * part
                square = part[:, 0:128]
                for j in range(1, width // 128):
                    square = square + part[:, j * 128 : (j + 1) * 128]
                squares[...] = squares[...] + square
            return carry

        if i == nz - 1:
            squares[...] = jnp.zeros_like(squares)

        lax.fori_loop(0, seg // width, body, 0)

    to_arrange = list(labels)
    to_add = list(labels)

    def work(arranges, adds):
        for _ in range(arranges):
            if to_arrange:
                arrange(to_arrange.pop(0))
        for _ in range(adds):
            while len(to_arrange) >= len(to_add):
                arrange(to_arrange.pop(0))
            add_chunk(to_add.pop(0))

    own_copy.wait()
    if ny > 1:
        @pl.when(y < ny - 1)
        def _():
            halo.wait_recv()
    for n, peer in firsts:
        start(remote(own.at[:, :, rim], gz[n].at[:, :, rim], z_send.at[n, 1], z_recv.at[n, 1], peer))
    start(remote(own.at[:, hi, rim], gx[0].at[:, :, rim], x_send.at[0, 1], x_recv.at[0, 1], opposite))
    swap(labels[0])
    w_copy.wait()
    work(EARLY, 0)
    for slot, peer in zip(slots, peers):
        remote(tab_v, tabs_v.at[slot], tab_send.at[0], tab_recv.at[slot], peer).wait_recv()
    to_smem = pltpu.make_async_copy(tabs_v, tabs_s, smem_sem)
    to_smem.start()
    to_smem.wait()
    near_tiles(labels[0])
    work(LATER, 0)

    by_hop = [[label for label in labels if label[1] == h] for h in range(nf + 1)]
    for h in range(1, nf + 1):
        for label in by_hop[h]:
            wait_z(label)
            pass_along(label)
            swap(label)
        if h < 3:
            work(1, 0)
        else:
            work(0, 1)
        for label in by_hop[h]:
            near_tiles(label)
        if h < 3:
            work(1, 0)
        else:
            work(0, 1)
        for label in by_hop[h - 1]:
            wait_hi(label)
            pass_along_hi(label)
            swap_hi(label)
        if h == 1:
            work(1, 0)
        if h == 2:
            work(0, 1)
        for label in by_hop[h - 1]:
            hi_tiles(label)
    for label in by_hop[nf]:
        wait_hi(label)
        swap_hi(label)
    while len(to_add) > len(by_hop[nf]):
        work(0, 1)
    for label in by_hop[nf]:
        hi_tiles(label)
        work(0, 1)

    block = 128
    for r in range(rows // block):
        part = squares[r * block : (r + 1) * block, :]
        ebuf[y, r : r + 1, :] = jnp.sum(part.T, axis=0, keepdims=True)

    for k, peer in enumerate(others):
        start(remote(ebuf.at[y], ebuf.at[y], y_send.at[k], y_recv.at[y], peer))
    for k in range(1, ny):
        source = lax.rem(y + k, ny)
        remote(ebuf.at[source], ebuf.at[source], y_send.at[0], y_recv.at[source], others[0]).wait_recv()
    energy = ebuf[0]
    for k in range(1, ny):
        energy = energy + ebuf[k]
    energy_ref[...] = energy
    for copy in sent:
        copy.wait_send()
    if ny > 1:
        @pl.when(y > 0)
        def _():
            halo.wait_send()


def classify(samples, energy_ref, cw_ref, cb_ref, lp_ref, lg_ref):
    log_power = jnp.log(energy_ref[...] / samples + 1e-06)
    per = SRC_BLOCK // 128
    for r in range(log_power.shape[0]):
        lp_ref[r // per : r // per + 1, (r % per) * 128 : (r % per + 1) * 128] = log_power[r : r + 1, :]
    powers = lp_ref[...]
    classes = cw_ref.shape[0]
    place = lax.broadcasted_iota(jnp.int32, (powers.shape[0], classes), 1)
    scores = jnp.broadcast_to(cb_ref[...], place.shape)
    for j in range(classes):
        score = jnp.sum(powers * cw_ref[j : j + 1, :], axis=1, keepdims=True)
        scores = scores + jnp.where(place == j, score, 0.0)
    lg_ref[...] = scores


def per_device(nz, ny, traces, stack_weights, channel_lists, lag_offsets, lengths, class_weights, class_bias):
    blocks = traces.shape[0] // BLOCK_CH
    seg = traces.shape[1]
    rows, depth = stack_weights.shape
    chunk = 2 * NX * BLOCK_CH
    bf16, f32 = jnp.bfloat16, jnp.float32
    vmem = pl.BlockSpec(memory_space=pltpu.VMEM)
    hbm = pl.BlockSpec(memory_space=pl.ANY)
    dma = pltpu.SemaphoreType.DMA
    width = min(seg, 256)
    whole = pltpu.VMEM((blocks, BLOCK_CH, seg + MAX_LAG), bf16)
    upper = pltpu.VMEM((blocks, HALF, seg + MAX_LAG), bf16)
    scratch = (
        [whole] * nz
        + [upper] * nz
        + [whole] * nz
        + [upper] * nz
        + [
            pltpu.VMEM((nz, 2 * NX, BLOCK_CH, seg), bf16),
            pltpu.VMEM((2 * nz, 2, BLOCK_CH, seg), bf16),
            pltpu.VMEM((nz, 2, HALF, seg), bf16),
            pltpu.VMEM((rows, depth), bf16),
            pltpu.VMEM((chunk, depth), bf16),
            pltpu.VMEM((nz, rows, chunk), bf16),
            pltpu.VMEM((seg // width, rows, width), f32),
            pltpu.VMEM((rows, 128), f32),
            pltpu.VMEM(channel_lists.shape, jnp.int32),
            pltpu.VMEM(channel_lists.shape, jnp.int32),
            pltpu.VMEM((1, 1), jnp.int32),
            pltpu.VMEM((8, 128), jnp.int32),
            pltpu.VMEM((8, 128), jnp.int32),
            pltpu.VMEM((4, 8, 128), jnp.int32),
            pltpu.SMEM((4, 8, 128), jnp.int32),
            pltpu.VMEM((ny, rows // 128, 128), f32),
            dma((5,)), dma((2,)), dma((3,)), dma((4,)), dma,
            dma((nz, 2)), dma((nz, 2)), dma((nz, 2)), dma((nz, 2)),
            dma((nz,)), dma((nz,)), dma((nz,)), dma((nz,)),
            dma((2 * nz,)), dma((nz,)), dma((nz, NX)), dma((ny,)), dma((ny,)),
        ]
    )
    energy = pl.pallas_call(
        functools.partial(kernel, nz, ny),
        out_shape=jax.ShapeDtypeStruct((rows // 128, 128), f32),
        in_specs=[hbm] * 5,
        out_specs=vmem,
        scratch_shapes=scratch,
        compiler_params=pltpu.CompilerParams(
            collective_id=0, has_side_effects=True, vmem_limit_bytes=56 * 1024 * 1024
        ),
    )(channel_lists, lag_offsets, lengths.reshape(1, 1), traces.reshape(blocks, BLOCK_CH, seg), stack_weights)
    return pl.pallas_call(
        functools.partial(classify, float(seg * ny)),
        out_shape=(
            jax.ShapeDtypeStruct((rows // SRC_BLOCK, SRC_BLOCK), f32),
            jax.ShapeDtypeStruct((rows // SRC_BLOCK, class_weights.shape[1]), f32),
        ),
        in_specs=[vmem] * 3,
        out_specs=(vmem, vmem),
    )(energy, class_weights.T, class_bias.reshape(1, -1))


def solution(mesh):
    placed = (
        P("fibre", "tm"),
        P("fibre", None),
        P("fibre", None),
        P("fibre", None),
        P("fibre"),
        P(),
        P(),
    )
    nz = mesh.shape["fibre"] // (2 * NX)
    return jax.shard_map(
        functools.partial(per_device, nz, mesh.shape["tm"]),
        mesh=mesh,
        in_specs=placed,
        out_specs=(P("fibre", None), P("fibre", None)),
        check_vma=False,
    )
```

```python
import functools

import jax
import jax.numpy as jnp
from jax import lax
from jax.experimental import pallas as pl
from jax.experimental.pallas import tpu as pltpu
from jax.sharding import PartitionSpec as P

BLOCK_CH = 32
MAX_LAG = 128
SRC_BLOCK = 256
NX = 4
HALF = BLOCK_CH // 2
EARLY, LATER = 1, 2
MESH = pl.DeviceIdType.MESH


def kernel(
    nz, ny, list_hbm, lag_hbm, len_hbm, traces_ref, w_ref, energy_ref, *scratch
):
    nf = nz // 2
    nb = nz - 1 - nf
    labels = [("o", 0)]
    for h in range(1, nf + 1):
        labels.append(("f", h))
        if h <= nb:
            labels.append(("b", h))
    at = {label: i for i, label in enumerate(labels)}
    gz = scratch[:nz]
    gx = scratch[nz : 2 * nz]
    gs = scratch[2 * nz : 3 * nz]
    gsx = scratch[3 * nz : 4 * nz]
    (
        tiles, full, half, w_v, perm_v, wp_v, acc, squares, list_ref, lag_ref, len_ref, pad, tab_v, tabs_v, tabs_s, ebuf,
        loc_sem, halo_sem, tab_send, tab_recv, smem_sem,
        z_send, z_recv, x_send, x_recv, s_send, s_recv, sx_send, sx_recv, f_send, h_send, t_recv, y_send, y_recv,
    ) = scratch[4 * nz :]
    seg = traces_ref.shape[2]
    rows = w_ref.shape[0]
    depth = w_ref.shape[1]
    count = list_ref.shape[1]
    chunk = 2 * NX * BLOCK_CH

    me = lax.axis_index("fibre")
    y = lax.axis_index("tm")
    c = lax.rem(me, 2)
    x = lax.rem(me // 2, NX)
    z = me // (2 * NX)
    d = 1 - 2 * c
    e = 1 - c

    def dev(zz, xx, cc):
        return {"fibre": (lax.rem(zz + 2 * nz, nz) * NX + lax.rem(xx + 2 * NX, NX)) * 2 + cc}

    def zoff(label):
        kind, h = label
        return {"o": 0, "f": -d * h, "b": d * h}[kind]

    def tslot(label):
        return lax.rem(zoff(label) + nz, nz)

    def col(xx, cc):
        return lax.rem(xx + 2 * NX, NX) * 2 + cc

    sibling = dev(z, x, e)
    peers = [dev(z, x + s, c) for s in (1, -1, 2)]
    slots = [2, 1, 3]
    opposite = peers[2]
    zfore, zback = dev(z + d, x, c), dev(z - d, x, c)
    ring = [zfore, zback] if nb else [zfore]
    others = [{"tm": lax.rem(y + k, ny)} for k in range(1, ny)]

    fetched = [
        pltpu.make_async_copy(src, dst, loc_sem.at[2 + i])
        for i, (src, dst) in enumerate(((list_hbm, list_ref), (lag_hbm, lag_ref), (len_hbm, len_ref)))
    ]
    for copy in fetched:
        copy.start()
    own = gz[0]
    hi = pl.ds(HALF, HALF)
    main, rim = pl.ds(0, seg), pl.ds(seg, MAX_LAG)
    own_copy = pltpu.make_async_copy(traces_ref, own.at[:, :, main], loc_sem.at[0])
    own_copy.start()
    w_copy = pltpu.make_async_copy(w_ref, w_v, loc_sem.at[1])
    w_copy.start()
    barrier = pltpu.get_barrier_semaphore()
    near = [sibling] + peers + ring
    for peer in near + others:
        pl.semaphore_signal(barrier, inc=1, device_id=peer, device_id_type=MESH)
    for copy in fetched:
        copy.wait()
    pad[...] = jnp.zeros_like(pad)
    pad[0:1, 0:count] = list_ref[...] + 256 * lag_ref[...]
    asked = jnp.broadcast_to(pad[0:1, :], (128, 128)).T[0:count, :]
    owner_of = lax.shift_right_logical(lax.bitwise_and(asked, 255), 2)
    word = lax.bitwise_or(
        lax.bitwise_and(asked, 3), lax.shift_left(lax.shift_right_logical(asked, 8), 2)
    )
    wanted = lax.broadcasted_iota(jnp.int32, (count, 128), 1)
    table = jnp.sum(jnp.where(owner_of == wanted, word, 0), axis=0, keepdims=True)
    tab_v[...] = jnp.broadcast_to(table, (8, 128))
    tabs_v[0] = tab_v[...]
    live = lax.broadcasted_iota(jnp.int32, (1, count), 1) < len_ref[...]
    keyed = jnp.where(live, lax.shift_right_logical(list_ref[...], 2), 2 * nz * NX)
    spread = lax.shift_right_logical(lax.broadcasted_iota(jnp.int32, (count, depth), 1), 5)
    spread = spread == lax.broadcasted_iota(jnp.int32, (count, depth), 0)
    key = jnp.dot(
        jnp.broadcast_to(keyed, (8, count)).astype(jnp.float32).astype(jnp.bfloat16),
        jnp.where(spread, 1.0, 0.0).astype(jnp.bfloat16),
        preferred_element_type=jnp.float32,
    )
    inner = lax.bitwise_and(lax.broadcasted_iota(jnp.int32, (1, depth), 1), BLOCK_CH - 1)
    key = key[0:1, :].astype(jnp.int32) * BLOCK_CH + inner

    @pl.when(y == ny - 1)
    def _():
        own[:, :, seg:] = jnp.zeros((own.shape[0], BLOCK_CH, MAX_LAG), jnp.bfloat16)

    pl.semaphore_wait(barrier, len(near) + len(others))

    def remote(src, dst, ssem, rsem, device):
        return pltpu.make_async_remote_copy(
            src_ref=src, dst_ref=dst, send_sem=ssem, recv_sem=rsem, device_id=device, device_id_type=MESH
        )

    sent = []

    def start(copy):
        copy.start()
        sent.append(copy)

    halo = remote(
        traces_ref.at[:, :, pl.ds(0, MAX_LAG)], own.at[:, :, rim],
        halo_sem.at[0], halo_sem.at[1], {"tm": lax.rem(y + ny - 1, ny)},
    )
    if ny > 1:
        @pl.when(y > 0)
        def _():
            halo.start()
    firsts = [(at[("f", 1)], zfore)] + ([(at[("b", 1)], zback)] if nb else [])
    for n, peer in firsts:
        start(remote(traces_ref, gz[n].at[:, :, main], z_send.at[n, 0], z_recv.at[n, 0], peer))
    start(remote(traces_ref.at[:, hi], gx[0].at[:, :, main], x_send.at[0, 0], x_recv.at[0, 0], opposite))
    for i, (slot, peer) in enumerate(zip(slots, peers)):
        start(remote(tab_v, tabs_v.at[slot], tab_send.at[i], tab_recv.at[slot], peer))

    def arrange(label):
        i = at[label]
        first = lax.rem(z + zoff(label) + nz, nz) * chunk
        target = lax.broadcasted_iota(jnp.int32, (chunk, chunk), 0) + first
        for kk in range(depth // chunk):
            hit = key[:, kk * chunk : (kk + 1) * chunk] == target
            perm_v[:, kk * chunk : (kk + 1) * chunk] = jnp.where(hit, 1.0, 0.0).astype(jnp.bfloat16)
        step = min(rows, 1024)

        def body(r, carry):
            at_row = pl.multiple_of(r * step, step)
            wp_v[i, pl.ds(at_row, step), :] = lax.dot_general(
                w_v[pl.ds(at_row, step), :], perm_v[...], (((1,), (1,)), ((), ())),
                preferred_element_type=jnp.float32,
            ).astype(jnp.bfloat16)
            return carry

        lax.fori_loop(0, rows // step, body, 0)

    def pass_along(label):
        kind, h = label
        i = at[label]
        if kind == "f" and h < nf:
            n = at[("f", h + 1)]
            start(remote(gz[i], gz[n], z_send.at[n, 0], z_recv.at[n, 0], zfore))
        if kind == "b" and h < nb:
            n = at[("b", h + 1)]
            start(remote(gz[i], gz[n], z_send.at[n, 0], z_recv.at[n, 0], zback))

    def pass_along_hi(label):
        kind, h = label
        i = at[label]
        if kind in "of" and h < nf:
            n = at[("f", h + 1)]
            start(remote(gx[i], gx[n], x_send.at[n, 0], x_recv.at[n, 0], zfore))
        if kind in "ob" and h < nb:
            n = at[("b", h + 1)]
            start(remote(gx[i], gx[n], x_send.at[n, 0], x_recv.at[n, 0], zback))

    def cut(src, height, region, owner, dst):
        lane = lax.broadcasted_iota(jnp.int32, (height, MAX_LAG), 1)
        word = tabs_s[region, 0, owner]
        block = lax.bitwise_and(word, 3)
        lag = lax.shift_right_logical(word, 2)
        turn = lax.bitwise_and(MAX_LAG - lag, MAX_LAG - 1)
        near = lane < MAX_LAG - lag
        held = pltpu.roll(src[block, 0:height, 0:MAX_LAG].astype(jnp.float32), turn, 1)
        for j in range(seg // MAX_LAG):
            following = pltpu.roll(
                src[block, 0:height, (j + 1) * MAX_LAG : (j + 2) * MAX_LAG].astype(jnp.float32), turn, 1
            )
            dst[:, j * MAX_LAG : (j + 1) * MAX_LAG] = jnp.where(near, held, following).astype(jnp.bfloat16)
            held = following

    def mirror(label):
        kind, h = label
        return {"o": ("o", 0), "f": ("b", h) if h <= nb else ("f", h), "b": ("f", h)}[kind]

    def swap(label):
        i = at[label]
        start(remote(gz[i], gs[i], s_send.at[i], s_recv.at[i], sibling))

    def swap_hi(label):
        i = at[label]
        start(remote(gx[i], gsx[i], sx_send.at[i], sx_recv.at[i], sibling))

    def near_tiles(label):
        i = at[label]
        t = tslot(label)
        m = at[mirror(label)]
        remote(gs[m], gs[m], s_send.at[m], s_recv.at[m], sibling).wait_recv()
        first = lax.rem(z + zoff(label) + nz, nz) * 2 * NX + 2 * x
        mine = pl.ds(2 * x, 2)
        for j in range(2):
            n = 2 * i + j
            cut(gz[i], BLOCK_CH, 1 + j, first + c, full.at[n, c])
            cut(gs[m], BLOCK_CH, 1 + j, first + e, full.at[n, e])
            start(remote(full.at[n], tiles.at[t, mine], f_send.at[n], t_recv.at[t, x], peers[j]))
        cut(gz[i], HALF, 3, first + c, half.at[i, c])
        cut(gs[m], HALF, 3, first + e, half.at[i, e])
        start(remote(half.at[i], tiles.at[t, mine, pl.ds(0, HALF)], h_send.at[i], t_recv.at[t, x], opposite))
        cut(gz[i], BLOCK_CH, 0, first + c, tiles.at[t, 2 * x + c])
        cut(gs[m], BLOCK_CH, 0, first + e, tiles.at[t, 2 * x + e])

    def hi_tiles(label):
        i = at[label]
        t = tslot(label)
        m = at[mirror(label)]
        remote(gsx[m], gsx[m], sx_send.at[m], sx_recv.at[m], sibling).wait_recv()
        there = col(x + 2, 0)
        first = lax.rem(z + zoff(label) + nz, nz) * 2 * NX + there
        cut(gx[i], HALF, 0, first + c, tiles.at[t, there + c, hi])
        cut(gsx[m], HALF, 0, first + e, tiles.at[t, there + e, hi])

    def wait_z(label):
        i = at[label]
        if label[1] == 1:
            for part, cols in enumerate((main, rim)):
                dst = gz[i].at[:, :, cols]
                remote(dst, dst, z_send.at[i, part], z_recv.at[i, part], zfore).wait_recv()
        else:
            remote(gz[i], gz[i], z_send.at[i, 0], z_recv.at[i, 0], zfore).wait_recv()

    def wait_hi(label):
        i = at[label]
        if label[1] == 0:
            for part, cols in enumerate((main, rim)):
                dst = gx[i].at[:, :, cols]
                remote(dst, dst, x_send.at[i, part], x_recv.at[i, part], zfore).wait_recv()
        else:
            remote(gx[i], gx[i], x_send.at[i, 0], x_recv.at[i, 0], zfore).wait_recv()

    def wait_tiles(label):
        t = tslot(label)
        for step in (1, -1):
            source = lax.rem(x + step + NX, NX)
            dst = tiles.at[t, pl.ds(2 * source, 2)]
            remote(full.at[0], dst, f_send.at[0], t_recv.at[t, source], sibling).wait_recv()
        source = lax.rem(x + 2, NX)
        dst = tiles.at[t, pl.ds(2 * source, 2), pl.ds(0, HALF)]
        remote(half.at[0], dst, h_send.at[0], t_recv.at[t, source], sibling).wait_recv()

    width = min(seg, 256)

    def add_chunk(*group):
        i = at[group[-1]]
        for label in group:
            wait_tiles(label)

        def body(n, carry):
            cols = pl.ds(pl.multiple_of(n * width, width), width)
            part = sum(
                jnp.dot(
                    wp_v[at[label]], tiles[tslot(label), :, :, cols].reshape(chunk, width),
                    preferred_element_type=jnp.float32,
                )
                for label in group
            )
            if at[group[0]] > 0:
                part = acc[n] + part
            if i < nz - 1:
                acc[n] = part
            else:
                part = part * part
                square = part[:, 0:128]
                for j in range(1, width // 128):
                    square = square + part[:, j * 128 : (j + 1) * 128]
                squares[...] = squares[...] + square
            return carry

        if i == nz - 1:
            squares[...] = jnp.zeros_like(squares)

        lax.fori_loop(0, seg // width, body, 0)

    to_arrange = list(labels)
    to_add = list(labels)

    def work(arranges, adds):
        for _ in range(arranges):
            if to_arrange:
                arrange(to_arrange.pop(0))
        group = [to_add.pop(0) for _ in range(adds)]
        while group and len(to_arrange) > len(to_add):
            arrange(to_arrange.pop(0))
        if group:
            add_chunk(*group)

    own_copy.wait()
    if ny > 1:
        @pl.when(y < ny - 1)
        def _():
            halo.wait_recv()
    for n, peer in firsts:
        start(remote(own.at[:, :, rim], gz[n].at[:, :, rim], z_send.at[n, 1], z_recv.at[n, 1], peer))
    start(remote(own.at[:, hi, rim], gx[0].at[:, :, rim], x_send.at[0, 1], x_recv.at[0, 1], opposite))
    swap(labels[0])
    w_copy.wait()
    work(EARLY, 0)
    for slot, peer in zip(slots, peers):
        remote(tab_v, tabs_v.at[slot], tab_send.at[0], tab_recv.at[slot], peer).wait_recv()
    to_smem = pltpu.make_async_copy(tabs_v, tabs_s, smem_sem)
    to_smem.start()
    to_smem.wait()
    near_tiles(labels[0])
    work(LATER, 0)

    by_hop = [[label for label in labels if label[1] == h] for h in range(nf + 1)]
    for h in range(1, nf + 1):
        for label in by_hop[h]:
            wait_z(label)
            pass_along(label)
            swap(label)
        if h <= 2:
            work(1, 0)
        for label in by_hop[h]:
            near_tiles(label)
        if h <= 2:
            work(1, 0)
        if h > 2:
            work(0, len(by_hop[h - 2]))
        for label in by_hop[h - 1]:
            wait_hi(label)
            pass_along_hi(label)
            swap_hi(label)
        if h == 1:
            work(1, 0)
        if h == 2:
            work(0, 1)
        for label in by_hop[h - 1]:
            hi_tiles(label)
    for label in by_hop[nf]:
        wait_hi(label)
        swap_hi(label)
    while len(to_add) > len(by_hop[nf]):
        work(0, min(2, len(to_add) - len(by_hop[nf])))
    for label in by_hop[nf]:
        hi_tiles(label)
        work(0, 1)

    block = 128
    for r in range(rows // block):
        part = squares[r * block : (r + 1) * block, :]
        ebuf[y, r : r + 1, :] = jnp.sum(part.T, axis=0, keepdims=True)

    for k, peer in enumerate(others):
        start(remote(ebuf.at[y], ebuf.at[y], y_send.at[k], y_recv.at[y], peer))
    for k in range(1, ny):
        source = lax.rem(y + k, ny)
        remote(ebuf.at[source], ebuf.at[source], y_send.at[0], y_recv.at[source], others[0]).wait_recv()
    energy = ebuf[0]
    for k in range(1, ny):
        energy = energy + ebuf[k]
    energy_ref[...] = energy
    for copy in sent:
        copy.wait_send()
    if ny > 1:
        @pl.when(y > 0)
        def _():
            halo.wait_send()


def classify(samples, energy_ref, cw_ref, cb_ref, lp_ref, lg_ref):
    log_power = jnp.log(energy_ref[...] / samples + 1e-06)
    per = SRC_BLOCK // 128
    for r in range(log_power.shape[0]):
        lp_ref[r // per : r // per + 1, (r % per) * 128 : (r % per + 1) * 128] = log_power[r : r + 1, :]
    powers = lp_ref[...]
    classes = cw_ref.shape[0]
    place = lax.broadcasted_iota(jnp.int32, (powers.shape[0], classes), 1)
    scores = jnp.broadcast_to(cb_ref[...], place.shape)
    for j in range(classes):
        score = jnp.sum(powers * cw_ref[j : j + 1, :], axis=1, keepdims=True)
        scores = scores + jnp.where(place == j, score, 0.0)
    lg_ref[...] = scores


def per_device(nz, ny, traces, stack_weights, channel_lists, lag_offsets, lengths, class_weights, class_bias):
    blocks = traces.shape[0] // BLOCK_CH
    seg = traces.shape[1]
    rows, depth = stack_weights.shape
    chunk = 2 * NX * BLOCK_CH
    bf16, f32 = jnp.bfloat16, jnp.float32
    vmem = pl.BlockSpec(memory_space=pltpu.VMEM)
    hbm = pl.BlockSpec(memory_space=pl.ANY)
    dma = pltpu.SemaphoreType.DMA
    width = min(seg, 256)
    whole = pltpu.VMEM((blocks, BLOCK_CH, seg + MAX_LAG), bf16)
    upper = pltpu.VMEM((blocks, HALF, seg + MAX_LAG), bf16)
    scratch = (
        [whole] * nz
        + [upper] * nz
        + [whole] * nz
        + [upper] * nz
        + [
            pltpu.VMEM((nz, 2 * NX, BLOCK_CH, seg), bf16),
            pltpu.VMEM((2 * nz, 2, BLOCK_CH, seg), bf16),
            pltpu.VMEM((nz, 2, HALF, seg), bf16),
            pltpu.VMEM((rows, depth), bf16),
            pltpu.VMEM((chunk, depth), bf16),
            pltpu.VMEM((nz, rows, chunk), bf16),
            pltpu.VMEM((seg // width, rows, width), f32),
            pltpu.VMEM((rows, 128), f32),
            pltpu.VMEM(channel_lists.shape, jnp.int32),
            pltpu.VMEM(channel_lists.shape, jnp.int32),
            pltpu.VMEM((1, 1), jnp.int32),
            pltpu.VMEM((8, 128), jnp.int32),
            pltpu.VMEM((8, 128), jnp.int32),
            pltpu.VMEM((4, 8, 128), jnp.int32),
            pltpu.SMEM((4, 8, 128), jnp.int32),
            pltpu.VMEM((ny, rows // 128, 128), f32),
            dma((5,)), dma((2,)), dma((3,)), dma((4,)), dma,
            dma((nz, 2)), dma((nz, 2)), dma((nz, 2)), dma((nz, 2)),
            dma((nz,)), dma((nz,)), dma((nz,)), dma((nz,)),
            dma((2 * nz,)), dma((nz,)), dma((nz, NX)), dma((ny,)), dma((ny,)),
        ]
    )
    energy = pl.pallas_call(
        functools.partial(kernel, nz, ny),
        out_shape=jax.ShapeDtypeStruct((rows // 128, 128), f32),
        in_specs=[hbm] * 5,
        out_specs=vmem,
        scratch_shapes=scratch,
        compiler_params=pltpu.CompilerParams(
            collective_id=0, has_side_effects=True, vmem_limit_bytes=56 * 1024 * 1024
        ),
    )(channel_lists, lag_offsets, lengths.reshape(1, 1), traces.reshape(blocks, BLOCK_CH, seg), stack_weights)
    return pl.pallas_call(
        functools.partial(classify, float(seg * ny)),
        out_shape=(
            jax.ShapeDtypeStruct((rows // SRC_BLOCK, SRC_BLOCK), f32),
            jax.ShapeDtypeStruct((rows // SRC_BLOCK, class_weights.shape[1]), f32),
        ),
        in_specs=[vmem] * 3,
        out_specs=(vmem, vmem),
    )(energy, class_weights.T, class_bias.reshape(1, -1))


def solution(mesh):
    placed = (
        P("fibre", "tm"),
        P("fibre", None),
        P("fibre", None),
        P("fibre", None),
        P("fibre"),
        P(),
        P(),
    )
    nz = mesh.shape["fibre"] // (2 * NX)
    return jax.shard_map(
        functools.partial(per_device, nz, mesh.shape["tm"]),
        mesh=mesh,
        in_specs=placed,
        out_specs=(P("fibre", None), P("fibre", None)),
        check_vma=False,
    )
```

```python
import functools

import jax
import jax.numpy as jnp
from jax import lax
from jax.experimental import pallas as pl
from jax.experimental.pallas import tpu as pltpu
from jax.sharding import PartitionSpec as P

BLOCK_CH = 32
MAX_LAG = 128
SRC_BLOCK = 256
NX = 4
HALF = BLOCK_CH // 2
EARLY, LATER = 1, 2
MESH = pl.DeviceIdType.MESH


def kernel(
    nz, ny, list_hbm, lag_hbm, len_hbm, traces_ref, w_ref, energy_ref, *scratch
):
    nf = nz // 2
    nb = nz - 1 - nf
    labels = [("o", 0)]
    for h in range(1, nf + 1):
        labels.append(("f", h))
        if h <= nb:
            labels.append(("b", h))
    at = {label: i for i, label in enumerate(labels)}
    gz = scratch[:nz]
    gx = scratch[nz : 2 * nz]
    gs = scratch[2 * nz : 3 * nz]
    gsx = scratch[3 * nz : 4 * nz]
    (
        tiles, full, half, w_v, perm_v, wp_v, acc, squares, list_ref, lag_ref, len_ref, pad, tab_v, tabs_v, tabs_s, ebuf,
        loc_sem, halo_sem, tab_send, tab_recv, smem_sem,
        z_send, z_recv, x_send, x_recv, s_send, s_recv, sx_send, sx_recv, f_send, h_send, t_recv, y_send, y_recv,
    ) = scratch[4 * nz :]
    seg = traces_ref.shape[2]
    rows = w_ref.shape[0]
    depth = w_ref.shape[1]
    count = list_ref.shape[1]
    chunk = 2 * NX * BLOCK_CH

    me = lax.axis_index("fibre")
    y = lax.axis_index("tm")
    c = lax.rem(me, 2)
    x = lax.rem(me // 2, NX)
    z = me // (2 * NX)
    d = 1 - 2 * c
    e = 1 - c

    def dev(zz, xx, cc):
        return {"fibre": (lax.rem(zz + 2 * nz, nz) * NX + lax.rem(xx + 2 * NX, NX)) * 2 + cc}

    def zoff(label):
        kind, h = label
        return {"o": 0, "f": -d * h, "b": d * h}[kind]

    def tslot(label):
        return lax.rem(zoff(label) + nz, nz)

    def col(xx, cc):
        return lax.rem(xx + 2 * NX, NX) * 2 + cc

    sibling = dev(z, x, e)
    peers = [dev(z, x + s, c) for s in (1, -1, 2)]
    slots = [2, 1, 3]
    opposite = peers[2]
    zfore, zback = dev(z + d, x, c), dev(z - d, x, c)
    ring = [zfore, zback] if nb else [zfore]
    far_first = sorted(range(1, ny), key=lambda k: -min(k, ny - k))
    others = [{"tm": lax.rem(y + k, ny)} for k in far_first]

    fetched = [
        pltpu.make_async_copy(src, dst, loc_sem.at[2 + i])
        for i, (src, dst) in enumerate(((list_hbm, list_ref), (lag_hbm, lag_ref), (len_hbm, len_ref)))
    ]
    for copy in fetched:
        copy.start()
    own = gz[0]
    hi = pl.ds(HALF, HALF)
    main, rim = pl.ds(0, seg), pl.ds(seg, MAX_LAG)
    own_copy = pltpu.make_async_copy(traces_ref, own.at[:, :, main], loc_sem.at[0])
    own_copy.start()
    w_copy = pltpu.make_async_copy(w_ref, w_v, loc_sem.at[1])
    w_copy.start()
    barrier = pltpu.get_barrier_semaphore()
    near = [sibling] + peers + ring
    for peer in near + others:
        pl.semaphore_signal(barrier, inc=1, device_id=peer, device_id_type=MESH)
    for copy in fetched:
        copy.wait()
    pad[...] = jnp.zeros_like(pad)
    pad[0:1, 0:count] = list_ref[...] + 256 * lag_ref[...]
    asked = jnp.broadcast_to(pad[0:1, :], (128, 128)).T[0:count, :]
    owner_of = lax.shift_right_logical(lax.bitwise_and(asked, 255), 2)
    word = lax.bitwise_or(
        lax.bitwise_and(asked, 3), lax.shift_left(lax.shift_right_logical(asked, 8), 2)
    )
    wanted = lax.broadcasted_iota(jnp.int32, (count, 128), 1)
    table = jnp.sum(jnp.where(owner_of == wanted, word, 0), axis=0, keepdims=True)
    tab_v[...] = jnp.broadcast_to(table, (8, 128))
    tabs_v[0] = tab_v[...]
    live = lax.broadcasted_iota(jnp.int32, (1, count), 1) < len_ref[...]
    keyed = jnp.where(live, lax.shift_right_logical(list_ref[...], 2), 2 * nz * NX)
    spread = lax.shift_right_logical(lax.broadcasted_iota(jnp.int32, (count, depth), 1), 5)
    spread = spread == lax.broadcasted_iota(jnp.int32, (count, depth), 0)
    key = jnp.dot(
        jnp.broadcast_to(keyed, (8, count)).astype(jnp.float32).astype(jnp.bfloat16),
        jnp.where(spread, 1.0, 0.0).astype(jnp.bfloat16),
        preferred_element_type=jnp.float32,
    )
    inner = lax.bitwise_and(lax.broadcasted_iota(jnp.int32, (1, depth), 1), BLOCK_CH - 1)
    key = key[0:1, :].astype(jnp.int32) * BLOCK_CH + inner

    @pl.when(y == ny - 1)
    def _():
        own[:, :, seg:] = jnp.zeros((own.shape[0], BLOCK_CH, MAX_LAG), jnp.bfloat16)

    pl.semaphore_wait(barrier, len(near) + len(others))

    def remote(src, dst, ssem, rsem, device):
        return pltpu.make_async_remote_copy(
            src_ref=src, dst_ref=dst, send_sem=ssem, recv_sem=rsem, device_id=device, device_id_type=MESH
        )

    sent = []

    def start(copy):
        copy.start()
        sent.append(copy)

    halo = remote(
        traces_ref.at[:, :, pl.ds(0, MAX_LAG)], own.at[:, :, rim],
        halo_sem.at[0], halo_sem.at[1], {"tm": lax.rem(y + ny - 1, ny)},
    )
    if ny > 1:
        @pl.when(y > 0)
        def _():
            halo.start()
    firsts = [(at[("f", 1)], zfore)] + ([(at[("b", 1)], zback)] if nb else [])
    for n, peer in firsts:
        start(remote(traces_ref, gz[n].at[:, :, main], z_send.at[n, 0], z_recv.at[n, 0], peer))
    start(remote(traces_ref.at[:, hi], gx[0].at[:, :, main], x_send.at[0, 0], x_recv.at[0, 0], opposite))
    for i, (slot, peer) in enumerate(zip(slots, peers)):
        start(remote(tab_v, tabs_v.at[slot], tab_send.at[i], tab_recv.at[slot], peer))

    def arrange(label):
        i = at[label]
        first = lax.rem(z + zoff(label) + nz, nz) * chunk
        target = lax.broadcasted_iota(jnp.int32, (chunk, chunk), 0) + first
        for kk in range(depth // chunk):
            hit = key[:, kk * chunk : (kk + 1) * chunk] == target
            perm_v[:, kk * chunk : (kk + 1) * chunk] = jnp.where(hit, 1.0, 0.0).astype(jnp.bfloat16)
        step = min(rows, 1024)

        def body(r, carry):
            at_row = pl.multiple_of(r * step, step)
            wp_v[i, pl.ds(at_row, step), :] = lax.dot_general(
                w_v[pl.ds(at_row, step), :], perm_v[...], (((1,), (1,)), ((), ())),
                preferred_element_type=jnp.float32,
            ).astype(jnp.bfloat16)
            return carry

        lax.fori_loop(0, rows // step, body, 0)

    def pass_along(label):
        kind, h = label
        i = at[label]
        if kind == "f" and h < nf:
            n = at[("f", h + 1)]
            start(remote(gz[i], gz[n], z_send.at[n, 0], z_recv.at[n, 0], zfore))
        if kind == "b" and h < nb:
            n = at[("b", h + 1)]
            start(remote(gz[i], gz[n], z_send.at[n, 0], z_recv.at[n, 0], zback))

    def pass_along_hi(label):
        kind, h = label
        i = at[label]
        if kind in "of" and h < nf:
            n = at[("f", h + 1)]
            start(remote(gx[i], gx[n], x_send.at[n, 0], x_recv.at[n, 0], zfore))
        if kind in "ob" and h < nb:
            n = at[("b", h + 1)]
            start(remote(gx[i], gx[n], x_send.at[n, 0], x_recv.at[n, 0], zback))

    def cut(src, height, region, owner, dst):
        lane = lax.broadcasted_iota(jnp.int32, (height, MAX_LAG), 1)
        word = tabs_s[region, 0, owner]
        block = lax.bitwise_and(word, 3)
        lag = lax.shift_right_logical(word, 2)
        turn = lax.bitwise_and(MAX_LAG - lag, MAX_LAG - 1)
        near = lane < MAX_LAG - lag
        held = pltpu.roll(src[block, 0:height, 0:MAX_LAG].astype(jnp.float32), turn, 1)
        for j in range(seg // MAX_LAG):
            following = pltpu.roll(
                src[block, 0:height, (j + 1) * MAX_LAG : (j + 2) * MAX_LAG].astype(jnp.float32), turn, 1
            )
            dst[:, j * MAX_LAG : (j + 1) * MAX_LAG] = jnp.where(near, held, following).astype(jnp.bfloat16)
            held = following

    def mirror(label):
        kind, h = label
        return {"o": ("o", 0), "f": ("b", h) if h <= nb else ("f", h), "b": ("f", h)}[kind]

    def swap(label):
        i = at[label]
        start(remote(gz[i], gs[i], s_send.at[i], s_recv.at[i], sibling))

    def swap_hi(label):
        i = at[label]
        start(remote(gx[i], gsx[i], sx_send.at[i], sx_recv.at[i], sibling))

    def near_tiles(label):
        i = at[label]
        t = tslot(label)
        m = at[mirror(label)]
        remote(gs[m], gs[m], s_send.at[m], s_recv.at[m], sibling).wait_recv()
        first = lax.rem(z + zoff(label) + nz, nz) * 2 * NX + 2 * x
        mine = pl.ds(2 * x, 2)
        for j in range(2):
            n = 2 * i + j
            cut(gz[i], BLOCK_CH, 1 + j, first + c, full.at[n, c])
            cut(gs[m], BLOCK_CH, 1 + j, first + e, full.at[n, e])
            start(remote(full.at[n], tiles.at[t, mine], f_send.at[n], t_recv.at[t, x], peers[j]))
        cut(gz[i], HALF, 3, first + c, half.at[i, c])
        cut(gs[m], HALF, 3, first + e, half.at[i, e])
        start(remote(half.at[i], tiles.at[t, mine, pl.ds(0, HALF)], h_send.at[i], t_recv.at[t, x], opposite))
        cut(gz[i], BLOCK_CH, 0, first + c, tiles.at[t, 2 * x + c])
        cut(gs[m], BLOCK_CH, 0, first + e, tiles.at[t, 2 * x + e])

    def hi_tiles(label):
        i = at[label]
        t = tslot(label)
        m = at[mirror(label)]
        remote(gsx[m], gsx[m], sx_send.at[m], sx_recv.at[m], sibling).wait_recv()
        there = col(x + 2, 0)
        first = lax.rem(z + zoff(label) + nz, nz) * 2 * NX + there
        cut(gx[i], HALF, 0, first + c, tiles.at[t, there + c, hi])
        cut(gsx[m], HALF, 0, first + e, tiles.at[t, there + e, hi])

    def wait_z(label):
        i = at[label]
        if label[1] == 1:
            for part, cols in enumerate((main, rim)):
                dst = gz[i].at[:, :, cols]
                remote(dst, dst, z_send.at[i, part], z_recv.at[i, part], zfore).wait_recv()
        else:
            remote(gz[i], gz[i], z_send.at[i, 0], z_recv.at[i, 0], zfore).wait_recv()

    def wait_hi(label):
        i = at[label]
        if label[1] == 0:
            for part, cols in enumerate((main, rim)):
                dst = gx[i].at[:, :, cols]
                remote(dst, dst, x_send.at[i, part], x_recv.at[i, part], zfore).wait_recv()
        else:
            remote(gx[i], gx[i], x_send.at[i, 0], x_recv.at[i, 0], zfore).wait_recv()

    def wait_tiles(label):
        t = tslot(label)
        for step in (1, -1):
            source = lax.rem(x + step + NX, NX)
            dst = tiles.at[t, pl.ds(2 * source, 2)]
            remote(full.at[0], dst, f_send.at[0], t_recv.at[t, source], sibling).wait_recv()
        source = lax.rem(x + 2, NX)
        dst = tiles.at[t, pl.ds(2 * source, 2), pl.ds(0, HALF)]
        remote(half.at[0], dst, h_send.at[0], t_recv.at[t, source], sibling).wait_recv()

    width = min(seg, 256)

    def add_chunk(*group):
        i = at[group[-1]]
        for label in group:
            wait_tiles(label)

        def body(n, carry):
            cols = pl.ds(pl.multiple_of(n * width, width), width)
            part = sum(
                jnp.dot(
                    wp_v[at[label]], tiles[tslot(label), :, :, cols].reshape(chunk, width),
                    preferred_element_type=jnp.float32,
                )
                for label in group
            )
            if at[group[0]] > 0:
                part = acc[n] + part
            if i < nz - 1:
                acc[n] = part
            else:
                part = part * part
                square = part[:, 0:128]
                for j in range(1, width // 128):
                    square = square + part[:, j * 128 : (j + 1) * 128]
                squares[...] = squares[...] + square
            return carry

        if i == nz - 1:
            squares[...] = jnp.zeros_like(squares)

        lax.fori_loop(0, seg // width, body, 0)

    to_arrange = list(labels)
    to_add = list(labels)

    def work(arranges, adds):
        for _ in range(arranges):
            if to_arrange:
                arrange(to_arrange.pop(0))
        group = [to_add.pop(0) for _ in range(adds)]
        while group and len(to_arrange) > len(to_add):
            arrange(to_arrange.pop(0))
        if group:
            add_chunk(*group)

    own_copy.wait()
    if ny > 1:
        @pl.when(y < ny - 1)
        def _():
            halo.wait_recv()
    for n, peer in firsts:
        start(remote(own.at[:, :, rim], gz[n].at[:, :, rim], z_send.at[n, 1], z_recv.at[n, 1], peer))
    start(remote(own.at[:, hi, rim], gx[0].at[:, :, rim], x_send.at[0, 1], x_recv.at[0, 1], opposite))
    swap(labels[0])
    w_copy.wait()
    work(EARLY, 0)
    for slot, peer in zip(slots, peers):
        remote(tab_v, tabs_v.at[slot], tab_send.at[0], tab_recv.at[slot], peer).wait_recv()
    to_smem = pltpu.make_async_copy(tabs_v, tabs_s, smem_sem)
    to_smem.start()
    to_smem.wait()
    near_tiles(labels[0])
    work(LATER, 0)

    by_hop = [[label for label in labels if label[1] == h] for h in range(nf + 1)]
    for h in range(1, nf + 1):
        for label in by_hop[h]:
            wait_z(label)
            pass_along(label)
            swap(label)
        if h <= 2:
            work(1, 0)
        for label in by_hop[h]:
            near_tiles(label)
        if h <= 2:
            work(1, 0)
        if h > 2:
            work(0, len(by_hop[h - 2]))
        for label in by_hop[h - 1]:
            wait_hi(label)
            pass_along_hi(label)
            swap_hi(label)
        if h == 1:
            work(1, 0)
        if h == 2:
            work(0, 1)
        for label in by_hop[h - 1]:
            hi_tiles(label)
    for label in by_hop[nf]:
        wait_hi(label)
        swap_hi(label)
    while len(to_add) > len(by_hop[nf]):
        work(0, min(2, len(to_add) - len(by_hop[nf])))
    for label in by_hop[nf]:
        hi_tiles(label)
        work(0, 1)

    block = 128
    for r in range(rows // block):
        part = squares[r * block : (r + 1) * block, :]
        ebuf[y, r : r + 1, :] = jnp.sum(part.T, axis=0, keepdims=True)

    for k, peer in enumerate(others):
        start(remote(ebuf.at[y], ebuf.at[y], y_send.at[k], y_recv.at[y], peer))
    for k in range(1, ny):
        source = lax.rem(y + k, ny)
        remote(ebuf.at[source], ebuf.at[source], y_send.at[0], y_recv.at[source], others[0]).wait_recv()
    energy = ebuf[0]
    for k in range(1, ny):
        energy = energy + ebuf[k]
    energy_ref[...] = energy
    for copy in sent:
        copy.wait_send()
    if ny > 1:
        @pl.when(y > 0)
        def _():
            halo.wait_send()


def classify(samples, energy_ref, cw_ref, cb_ref, lp_ref, lg_ref):
    log_power = jnp.log(energy_ref[...] / samples + 1e-06)
    per = SRC_BLOCK // 128
    for r in range(log_power.shape[0]):
        lp_ref[r // per : r // per + 1, (r % per) * 128 : (r % per + 1) * 128] = log_power[r : r + 1, :]
    powers = lp_ref[...]
    classes = cw_ref.shape[0]
    place = lax.broadcasted_iota(jnp.int32, (powers.shape[0], classes), 1)
    scores = jnp.broadcast_to(cb_ref[...], place.shape)
    for j in range(classes):
        score = jnp.sum(powers * cw_ref[j : j + 1, :], axis=1, keepdims=True)
        scores = scores + jnp.where(place == j, score, 0.0)
    lg_ref[...] = scores


def per_device(nz, ny, traces, stack_weights, channel_lists, lag_offsets, lengths, class_weights, class_bias):
    blocks = traces.shape[0] // BLOCK_CH
    seg = traces.shape[1]
    rows, depth = stack_weights.shape
    chunk = 2 * NX * BLOCK_CH
    bf16, f32 = jnp.bfloat16, jnp.float32
    vmem = pl.BlockSpec(memory_space=pltpu.VMEM)
    hbm = pl.BlockSpec(memory_space=pl.ANY)
    dma = pltpu.SemaphoreType.DMA
    width = min(seg, 256)
    whole = pltpu.VMEM((blocks, BLOCK_CH, seg + MAX_LAG), bf16)
    upper = pltpu.VMEM((blocks, HALF, seg + MAX_LAG), bf16)
    scratch = (
        [whole] * nz
        + [upper] * nz
        + [whole] * nz
        + [upper] * nz
        + [
            pltpu.VMEM((nz, 2 * NX, BLOCK_CH, seg), bf16),
            pltpu.VMEM((2 * nz, 2, BLOCK_CH, seg), bf16),
            pltpu.VMEM((nz, 2, HALF, seg), bf16),
            pltpu.VMEM((rows, depth), bf16),
            pltpu.VMEM((chunk, depth), bf16),
            pltpu.VMEM((nz, rows, chunk), bf16),
            pltpu.VMEM((seg // width, rows, width), f32),
            pltpu.VMEM((rows, 128), f32),
            pltpu.VMEM(channel_lists.shape, jnp.int32),
            pltpu.VMEM(channel_lists.shape, jnp.int32),
            pltpu.VMEM((1, 1), jnp.int32),
            pltpu.VMEM((8, 128), jnp.int32),
            pltpu.VMEM((8, 128), jnp.int32),
            pltpu.VMEM((4, 8, 128), jnp.int32),
            pltpu.SMEM((4, 8, 128), jnp.int32),
            pltpu.VMEM((ny, rows // 128, 128), f32),
            dma((5,)), dma((2,)), dma((3,)), dma((4,)), dma,
            dma((nz, 2)), dma((nz, 2)), dma((nz, 2)), dma((nz, 2)),
            dma((nz,)), dma((nz,)), dma((nz,)), dma((nz,)),
            dma((2 * nz,)), dma((nz,)), dma((nz, NX)), dma((ny,)), dma((ny,)),
        ]
    )
    energy = pl.pallas_call(
        functools.partial(kernel, nz, ny),
        out_shape=jax.ShapeDtypeStruct((rows // 128, 128), f32),
        in_specs=[hbm] * 5,
        out_specs=vmem,
        scratch_shapes=scratch,
        compiler_params=pltpu.CompilerParams(
            collective_id=0, has_side_effects=True, vmem_limit_bytes=56 * 1024 * 1024
        ),
    )(channel_lists, lag_offsets, lengths.reshape(1, 1), traces.reshape(blocks, BLOCK_CH, seg), stack_weights)
    return pl.pallas_call(
        functools.partial(classify, float(seg * ny)),
        out_shape=(
            jax.ShapeDtypeStruct((rows // SRC_BLOCK, SRC_BLOCK), f32),
            jax.ShapeDtypeStruct((rows // SRC_BLOCK, class_weights.shape[1]), f32),
        ),
        in_specs=[vmem] * 3,
        out_specs=(vmem, vmem),
    )(energy, class_weights.T, class_bias.reshape(1, -1))


def solution(mesh):
    placed = (
        P("fibre", "tm"),
        P("fibre", None),
        P("fibre", None),
        P("fibre", None),
        P("fibre"),
        P(),
        P(),
    )
    nz = mesh.shape["fibre"] // (2 * NX)
    return jax.shard_map(
        functools.partial(per_device, nz, mesh.shape["tm"]),
        mesh=mesh,
        in_specs=placed,
        out_specs=(P("fibre", None), P("fibre", None)),
        check_vma=False,
    )
```
